128 devices in a mesh: dp: 32 (over x_lo, z, y), tensor: 4 (over x_hi, core).
Axes of the slice: x: 4 (x_hi: 2, x_lo: 2; x = x_hi * 2 + x_lo), y: 4, z: 4, core: 2. Of those that a mesh axis runs over, the one named last changes fastest.
Arguments:
- token_ids: int32 [4, 256], replicated, may hold values from 0 to 75967
- embed_table: bfloat16 [75968, 4096], P('dp', 'tensor'), may hold values from -6 to 6
- norm_gain: float32 [4096], replicated, may hold values from 0.25 to 1.75
- query_gain: float32 [128], replicated, may hold values from 0.25 to 1.75
- key_gain: float32 [128], replicated, may hold values from 0.25 to 1.75
- base_query_weight: bfloat16 [4096, 4096], P(None, 'tensor'), may hold values from -0.09375 to 0.09375
- pair_weight: bfloat16 [2, 4096, 256], replicated, may hold values from -0.09375 to 0.09375
- past_pairs: bfloat16 [256, 512, 2, 256], P('dp'), may hold values from -96 to 96
- down_factor: float32 [64, 4096], P('dp'), may hold values from -6 to 6
- up_factor: float32 [64, 4096], P('dp', 'tensor'), may hold values from -6 to 6
- grad_down: bfloat16 [32, 64, 4096], P('dp'), may hold values from -200 to 200
- grad_up: bfloat16 [32, 64, 4096], P('dp', None, 'tensor'), may hold values from -200 to 200
- group_scale: float32 [32], replicated, may hold values from 0.25 to 4
- learner_group: int32 [32], replicated, may hold values from 0 to 31, each once
Outputs:
- attended: bfloat16 [4, 256, 4096], P(None, 'dp', 'tensor')
- new_down: float32 [64, 4096], P('dp')
- new_up: float32 [64, 4096], P('dp', 'tensor')
The draws below stay inside these ranges and needn't reach their ends.
Inputs may be any that keep to these rules, and one draw needn't show every extreme that they name: `learner_group`: each learner processed exactly one rollout group, each group exactly once.
All inputs are finite; a program needn't handle non-finite values.
Results may differ from the reference program's by a relative error of at most 0.012.
The reference program's roundings to bfloat16 on the way count: a program that leaves them out, or rounds other values in their place, can miss the bound.
Values may be sent and summed in bfloat16 or wider, within the bound.
No kernel may reach another device: no remote copies, remote signals or barrier semaphores. Data moves between devices by JAX's collectives and lax.ppermute only.
A program may use at most 128 MiB of HBM per device.

```python
import math
import jax
import jax.numpy as jnp
import numpy as np
from jax import lax

D = 4096
HEAD = 128
HEADS = 32
KVH = 2
R = 64
VOCAB = 75968
STEPS = 4
CTX = 512
HD = 4096
GROUP_ROWS = 256
N_DP = 32


def draw_past_pairs(key, part):
    key = jax.random.fold_in(key, 11)
    first = jax.random.fold_in(key, 0)
    shape = (GROUP_ROWS, CTX, KVH, 2 * HEAD)
    base = jnp.clip(jax.random.normal(first, shape, jnp.float32), -6.0, 6.0)
    return base.astype(jnp.bfloat16)


def rising_gradient(key, columns, row_rise, column_rise):
    first = jax.random.fold_in(key, 0)
    shape = (N_DP, R, columns)
    own = jnp.clip(jax.random.normal(first, shape, jnp.float32), -6.0, 6.0)
    base = own
    row_pos = jnp.arange(R, dtype=jnp.float32) / max(R - 1, 1)
    col_pos = jnp.arange(columns, dtype=jnp.float32) / max(columns - 1, 1)
    row_scale = jnp.exp(math.log(row_rise) * row_pos)[None, :, None]
    col_scale = jnp.exp(math.log(column_rise) * col_pos)[None, None, :]
    return jnp.clip(base * row_scale * col_scale, -200.0, 200.0)


def draw_grad_down(key, part):
    key = jax.random.fold_in(key, 23)
    values = rising_gradient(key, D, 8.0, 3.0)
    return values.astype(jnp.bfloat16)


def draw_grad_up(key, part):
    key = jax.random.fold_in(key, 37)
    values = rising_gradient(key, HD, 8.0, 3.0)
    return values.astype(jnp.bfloat16)


def set_ends(entries, stream_key, least, top_value):
    longest = entries.shape.index(max(entries.shape))
    spots = []
    for shift in (0, 1):
        where = [jax.random.randint(jax.random.fold_in(stream_key, axis), (), 0, length) for axis, length in enumerate(entries.shape)]
        where[longest] = (where[longest] + shift) % entries.shape[longest]
        spots.append(tuple(where))
    return entries.at[spots[0]].set(least).at[spots[1]].set(top_value)


def shard_levels(rng, extent, pieces, low, largest):
    factor_of, own = 1.0, jax.random.fold_in(rng, 6)
    for axis_at, parts in pieces:
        draws = jnp.exp(jax.random.uniform(jax.random.fold_in(own, axis_at), (parts,), jnp.float32, low / len(pieces), largest / len(pieces)))
        factor_of = factor_of * jnp.repeat(draws, extent[axis_at] // parts).reshape([-1 if axis == axis_at else 1 for axis in range(len(extent))])
    return factor_of


def skewed_wide(own_key, extent, count, skew):
    portions = [min(1 << octave, count + 1 - (1 << octave)) * (1 << 20) // math.isqrt((1 << octave) ** skew) + 1 for octave in range((count + 1).bit_length()) if 1 << octave <= count]
    deviation = 1 + sum(portions) // (1 << 30)
    grid = np.cumsum(np.array([max(1, weight // deviation) for weight in portions]))
    pick = jax.random.randint(jax.random.fold_in(own_key, 1), extent, 0, int(grid[len(portions) - 1]))
    start = jnp.left_shift(1, jnp.searchsorted(jnp.asarray(grid, jnp.int32), pick, side="right").astype(jnp.int32))
    standing = start - 1 + jax.random.randint(jax.random.fold_in(own_key, 4), extent, 0, 1 << 30) % jnp.minimum(start, count + 1 - start)
    return jax.random.permutation(jax.random.fold_in(own_key, 2), count)[standing].astype(jnp.int32)


def centred(stream_key, dims, width, most, cuts=(), held_as=jnp.bfloat16):
    entries = jax.random.normal(stream_key, dims, jnp.float32) * width
    if len(cuts) > 0:
        entries = shard_levels(stream_key, dims, cuts, -0.22, 0.18) * entries
    return jnp.clip(entries, min=-most, max=most).astype(held_as)


def setup_inputs(seed: int = 0) -> dict:
    key_list = jax.random.split(jax.random.key(seed), 15)
    token_ids = set_ends(skewed_wide(key_list[0], (STEPS, GROUP_ROWS), VOCAB, 2), jax.random.fold_in(key_list[0], 3), 0, VOCAB - 1).astype(jnp.int32)
    embed_table = centred(key_list[1], (VOCAB, D), 1.0, 6.0, ((0, 32), (1, 4)))
    norm_gain = jnp.clip(1.0 + 0.15 * jax.random.normal(key_list[2], (D,), jnp.float32), 0.25, 1.75)
    query_gain = jnp.clip(1.0 + 0.15 * jax.random.normal(key_list[3], (HEAD,), jnp.float32), 0.25, 1.75)
    key_gain = jnp.clip(1.0 + 0.15 * jax.random.normal(key_list[4], (HEAD,), jnp.float32), 0.25, 1.75)
    base_query_weight = centred(key_list[5], (D, HD), D ** -0.5, 0.09375, ((1, 4),))
    pair_weight = centred(key_list[6], (KVH, D, 2 * HEAD), D ** -0.5, 0.09375)
    past_pairs = draw_past_pairs(jax.random.fold_in(key_list[14], 71), 0)
    down_factor = centred(key_list[8], (R, D), 1.0, 6.0, ((0, 32),), jnp.float32)
    up_factor = centred(key_list[9], (R, HD), 1.0, 6.0, ((0, 32), (1, 4)), jnp.float32)
    grad_down = draw_grad_down(jax.random.fold_in(key_list[14], 71), 0)
    grad_up = draw_grad_up(jax.random.fold_in(key_list[14], 71), 0)
    group_scale = jnp.clip(jnp.exp(jax.random.uniform(key_list[12], (N_DP,), jnp.float32, math.log(0.25), math.log(4.0))), 0.25, 4.0)
    learner_group = jax.random.permutation(key_list[13], N_DP).astype(jnp.int32)
    return dict(token_ids=token_ids, embed_table=embed_table, norm_gain=norm_gain, query_gain=query_gain, key_gain=key_gain, base_query_weight=base_query_weight, pair_weight=pair_weight, past_pairs=past_pairs, down_factor=down_factor, up_factor=up_factor, grad_down=grad_down, grad_up=grad_up, group_scale=group_scale, learner_group=learner_group)


EPSILON = 1e-06
STEP_RATIO = 0.3
ADAPTER_SCALING = 1.0 / 1024.0

def normalize(values, gain):
    return values * lax.rsqrt(lax.optimization_barrier(jnp.mean(values * values, axis=-1, keepdims=True)) + EPSILON) * gain

def reference(token_ids, embed_table, norm_gain, query_gain, key_gain, base_query_weight, pair_weight, past_pairs, down_factor, up_factor, grad_down, grad_up, group_scale, learner_group):
    highest = lax.Precision.HIGHEST
    weight = group_scale[learner_group]
    sum_down = jnp.einsum('l,lrd->rd', weight, grad_down.astype(jnp.float32), precision=highest)
    up_factor_sum = jnp.einsum('l,lrd->rd', weight, grad_up.astype(jnp.float32), precision=highest)
    overall = jnp.sum(sum_down * sum_down) + jnp.sum(up_factor_sum * up_factor_sum)
    clip_coef = 1.0 / jnp.maximum(jnp.sqrt(overall), 1.0)
    rate = STEP_RATIO * math.sqrt(R * (D + HD))
    new_down = down_factor - rate * clip_coef * sum_down
    new_up = up_factor - rate * clip_coef * up_factor_sum
    weight_change = jnp.dot(new_down.T, new_up, precision=highest, preferred_element_type=jnp.float32)
    merged_weight = (base_query_weight.astype(jnp.float32) + ADAPTER_SCALING * weight_change).astype(jnp.bfloat16)
    heads_per_group = HEADS // KVH
    cached_keys = past_pairs[..., :HEAD].astype(jnp.float32)
    cached_values = past_pairs[..., HEAD:].astype(jnp.float32)
    inverse = 1.0 / math.sqrt(HEAD)
    fresh_keys = []
    fresh_values = []
    outputs = []
    for decode_step in range(STEPS):
        embedded = embed_table[token_ids[decode_step]]
        normed = normalize(embedded.astype(jnp.float32), norm_gain).astype(jnp.bfloat16)
        query = jnp.dot(normed, merged_weight, preferred_element_type=jnp.float32)
        query = query.reshape(GROUP_ROWS, KVH, heads_per_group, HEAD)
        query_normed = normalize(query, query_gain).astype(jnp.bfloat16).astype(jnp.float32)
        pairs = jnp.einsum('rd,kde->rke', normed.astype(jnp.float32), pair_weight.astype(jnp.float32))
        key_new = normalize(pairs[..., :HEAD], key_gain).astype(jnp.bfloat16)
        value_new = pairs[..., HEAD:].astype(jnp.bfloat16)
        fresh_keys.append(key_new)
        fresh_values.append(value_new)
        new_keys = jnp.stack(fresh_keys, axis=1).astype(jnp.float32)
        new_values = jnp.stack(fresh_values, axis=1).astype(jnp.float32)
        scores_old = jnp.einsum('rkgd,rckd->rkgc', query_normed, cached_keys) * inverse
        scores_new = jnp.einsum('rkgd,rckd->rkgc', query_normed, new_keys) * inverse
        scores = jnp.concatenate([scores_old, scores_new], axis=-1)
        top = lax.optimization_barrier(jnp.max(scores, axis=-1, keepdims=True))
        expo = jnp.exp(scores - top)
        probs = (expo / lax.optimization_barrier(jnp.sum(expo, axis=-1, keepdims=True))).astype(jnp.bfloat16).astype(jnp.float32)
        result = jnp.einsum('rkgc,rckd->rkgd', probs[..., :CTX], cached_values)
        result = result + jnp.einsum('rkgc,rckd->rkgd', probs[..., CTX:], new_values)
        outputs.append(result.astype(jnp.bfloat16).reshape(GROUP_ROWS, HD))
    return (jnp.stack(outputs), new_down, new_up)
```

```python
import functools
import math

import jax
import jax.numpy as jnp
from jax import lax
from jax.experimental import pallas as pl
from jax.experimental.pallas import tpu as pltpu
from jax.sharding import PartitionSpec as P

D = 4096
HEAD = 128
HEADS = 32
KVH = 2
R = 64
STEPS = 4
HD = 4096
CAP = 8

EPSILON = 1e-06
STEP_RATIO = 0.3
ADAPTER_SCALING = 1.0 / 1024.0
RATE = STEP_RATIO * math.sqrt(R * (D + HD))
VMEM_LIMIT = 48 * 1024 * 1024


def split(values):
    high = values.astype(jnp.bfloat16)
    return high, (values - high.astype(jnp.float32)).astype(jnp.bfloat16)


def dot_nt(a, b):
    return lax.dot_general(a, b, (((1,), (1,)), ((), ())), preferred_element_type=jnp.float32)


def dot_nn(a, b):
    return lax.dot_general(a, b, (((1,), (0,)), ((), ())), preferred_element_type=jnp.float32)


def plan_tokens(token_ids, groups, vocab_rows):
    steps, rows = token_ids.shape
    ids = token_ids.reshape(steps, groups, rows // groups).transpose(1, 0, 2)
    ids = ids.reshape(groups, steps * (rows // groups))
    count = ids.shape[1]
    earlier = jnp.arange(count)[None, :] < jnp.arange(count)[:, None]
    one, other = ids[:, :, None], ids[:, None, :]
    repeated = jnp.any((one == other) & earlier[None], axis=2)
    low = ids // vocab_rows * vocab_rows
    before = (other >= low[:, :, None]) & (other < one) & ~repeated[:, None, :]
    slot = jnp.sum(before.astype(jnp.int32), axis=2)
    return ids, slot


def own_rows(ids, slot, first_slot, embed_table):
    vocab_rows = embed_table.shape[0]
    local = ids - lax.axis_index("dp") * vocab_rows
    mine = (local >= 0) & (local < vocab_rows)
    wanted = slot[:, None, :] == first_slot + jnp.arange(CAP)[None, :, None]
    chosen = jnp.max(jnp.where(wanted & mine[:, None, :], local[:, None, :], -1), axis=2)
    one_hot = (chosen.reshape(-1, 1) == jnp.arange(vocab_rows)[None, :]).astype(jnp.bfloat16)
    found = dot_nn(one_hot, embed_table).astype(jnp.bfloat16)
    return found.reshape(ids.shape[0], CAP, -1)


def pick_rows(ids, slot, first_slot, vocab_rows, received):
    me = lax.axis_index("dp")
    own_ids = lax.dynamic_index_in_dim(ids, me, 0, keepdims=False)
    own_slot = lax.dynamic_index_in_dim(slot, me, 0, keepdims=False) - first_slot
    place = own_ids // vocab_rows * CAP + own_slot
    place = jnp.where((own_slot >= 0) & (own_slot < CAP), place, -1)
    columns = received.shape[0] * CAP
    one_hot = (place[:, None] == jnp.arange(columns)[None, :]).astype(jnp.bfloat16)
    return dot_nn(one_hot, received.reshape(columns, -1)).astype(jnp.bfloat16)


def project_kernel(place, e0, e1, e2, e3, gain, factors, normed, partial):
    t = place[0]
    blocks = [e[...].astype(jnp.float32) for e in (e0, e1, e2, e3)]
    square = sum(jnp.sum(b * b, axis=1, keepdims=True) for b in blocks)
    scale = lax.rsqrt(square / D + EPSILON)
    width = blocks[0].shape[1]
    own = None
    for k, block in enumerate(blocks):
        columns = pl.ds(pl.multiple_of((t ^ k) * width, width), width)
        value = (block * scale * gain[:, columns]).astype(jnp.bfloat16)
        normed[:, columns] = value
        own = value if k == 0 else own
    rows = factors[...].reshape(-1, width)
    high, low = split(rows)
    rows_at = lax.broadcasted_iota(jnp.int32, rows.shape, 0) % 8
    total = jnp.sum(jnp.where(rows_at < 4, rows * rows, 0.0))
    count = own.shape[0]
    partial[:count, :] = dot_nt(own, high) + dot_nt(own, low)
    partial[count:, :] = jnp.full((8, rows.shape[0]), total, jnp.float32)


def base_kernel(place, normed, base, pair, gain, query, key_new, value_new, pairs):
    step = pl.program_id(0)

    @pl.when(step == 0)
    def _():
        query[...] = jnp.zeros_like(query)
        pairs[...] = jnp.zeros_like(pairs)

    query[...] += dot_nn(normed[...], base[...])
    pairs[...] += dot_nn(normed[...], pair[0])

    @pl.when(step == pl.num_programs(0) - 1)
    def _():
        keys = pairs[:, :HEAD]
        scale = lax.rsqrt(jnp.mean(keys * keys, axis=1, keepdims=True) + EPSILON)
        key_new[...] = (keys * scale * gain[...]).astype(jnp.bfloat16)
        value_new[...] = pairs[:, HEAD:].astype(jnp.bfloat16)


def attend_kernel(
    place, base_query, products, factors, gain, key_new, value_new, cache, out, queries, results
):
    row = pl.program_id(0)
    row_count = pl.num_programs(0)
    pair_index = place[1]
    count, width = base_query.shape
    heads = width // HEAD
    per_row = count // 8 * heads

    @pl.when(row == 0)
    def _():
        sums = products[:count, :]
        overall = products[count : count + 1, :]
        clip = RATE / jnp.maximum(jnp.sqrt(overall), 1.0)
        lane = lax.broadcasted_iota(jnp.int32, sums.shape, 1) % 8
        updated = sums - clip * pltpu.roll(sums, 4, 1)
        updated = jnp.where((lane == 4) | (lane == 5), updated, 0.0)
        lanes = updated.shape[1]
        spread = pltpu.roll(updated, 2, 1) - clip * pltpu.roll(updated, lanes - 2, 1)
        rows = factors[...].reshape(-1, width)
        high, low = split(rows)
        left_high, left_low = split(spread)
        change = dot_nn(left_high, high) + dot_nn(left_low, high) + dot_nn(left_high, low)
        query = base_query[...] + ADAPTER_SCALING * change
        for h in range(heads):
            part = query[:, h * HEAD : (h + 1) * HEAD]
            scale = lax.rsqrt(jnp.mean(part * part, axis=1, keepdims=True) + EPSILON)
            part = (part * scale * gain[...]).astype(jnp.bfloat16).astype(jnp.float32)
            for s in range(count // 8):
                queries[pl.ds(s * heads + h, 8, stride=per_row), :] = part[s * 8 : s * 8 + 8]

    own = pl.ds(pl.multiple_of(row * per_row, per_row), per_row)
    query = queries[own, :].astype(jnp.bfloat16)
    inverse = 1.0 / math.sqrt(HEAD)
    pairs = cache[0]
    old = dot_nt(query, pairs) * inverse
    lane = lax.broadcasted_iota(jnp.int32, old.shape, 1) % 4
    old = jnp.where(lane == pair_index, old, -jnp.inf)
    new = dot_nt(query, key_new[...]) * inverse
    new_lane = lax.broadcasted_iota(jnp.int32, new.shape, 1)
    step = lax.broadcasted_iota(jnp.int32, new.shape, 0) // heads
    new = jnp.where((new_lane % 8 == row) & (new_lane // 8 <= step), new, -jnp.inf)
    top = jnp.maximum(jnp.max(old, axis=1, keepdims=True), jnp.max(new, axis=1, keepdims=True))
    old, new = jnp.exp(old - top), jnp.exp(new - top)
    total = jnp.sum(old, axis=1, keepdims=True) + jnp.sum(new, axis=1, keepdims=True)
    old = pltpu.roll(old / total, 2, 1).astype(jnp.bfloat16)
    new = (new / total).astype(jnp.bfloat16)
    results[own, :] = dot_nn(old, pairs) + dot_nn(new, value_new[...])

    @pl.when(row == row_count - 1)
    def _():
        for h in range(heads):
            parts = [
                results[pl.ds(s * heads + h, 8, stride=per_row), :] for s in range(count // 8)
            ]
            out[:, h * HEAD : (h + 1) * HEAD] = jnp.concatenate(parts, 0).astype(jnp.bfloat16)


def vmem():
    return pl.BlockSpec(memory_space=pltpu.VMEM)


def smem():
    return pl.BlockSpec(memory_space=pltpu.SMEM)


def project(place, blocks, gain, factors):
    count, width = blocks[0].shape
    return pl.pallas_call(
        project_kernel,
        out_shape=(
            jax.ShapeDtypeStruct((count, 4 * width), jnp.bfloat16),
            jax.ShapeDtypeStruct((count + 8, factors.shape[0] * factors.shape[1]), jnp.float32),
        ),
        in_specs=[smem()] + [vmem()] * 6,
        out_specs=(vmem(), vmem()),
        compiler_params=pltpu.CompilerParams(vmem_limit_bytes=VMEM_LIMIT),
        name="project",
    )(place, *blocks, gain.reshape(1, -1), factors)


def base_products(place, normed, base, pair, gain):
    count, depth = normed.shape
    width = base.shape[1]
    tile = 512
    spec = pltpu.PrefetchScalarGridSpec(
        num_scalar_prefetch=1,
        grid=(depth // tile,),
        in_specs=[
            pl.BlockSpec((count, tile), lambda i, place: (0, i)),
            pl.BlockSpec((tile, width), lambda i, place: (i, 0)),
            pl.BlockSpec((1, tile, 2 * HEAD), lambda i, place: (place[1], i, 0)),
            pl.BlockSpec((1, HEAD), lambda i, place: (0, 0)),
        ],
        out_specs=(
            pl.BlockSpec((count, width), lambda i, place: (0, 0)),
            pl.BlockSpec((count, HEAD), lambda i, place: (0, 0)),
            pl.BlockSpec((count, HEAD), lambda i, place: (0, 0)),
        ),
        scratch_shapes=[pltpu.VMEM((count, 2 * HEAD), jnp.float32)],
    )
    return pl.pallas_call(
        base_kernel,
        out_shape=(
            jax.ShapeDtypeStruct((count, width), jnp.float32),
            jax.ShapeDtypeStruct((count, HEAD), jnp.bfloat16),
            jax.ShapeDtypeStruct((count, HEAD), jnp.bfloat16),
        ),
        grid_spec=spec,
        compiler_params=pltpu.CompilerParams(vmem_limit_bytes=VMEM_LIMIT),
        cost_estimate=pl.CostEstimate(
            flops=2 * count * depth * width, bytes_accessed=2 * depth * width, transcendentals=0
        ),
        name="base_products",
    )(place, normed, base, pair, gain.reshape(1, -1))


def attend(place, base_query, products, factors, gain, key_new, value_new, cache):
    count, width = base_query.shape
    rows, entries, _ = cache.shape

    def whole(x):
        return pl.BlockSpec(x.shape, lambda i, place: (0,) * x.ndim)

    gain = gain.reshape(1, -1)
    spec = pltpu.PrefetchScalarGridSpec(
        num_scalar_prefetch=1,
        grid=(rows,),
        in_specs=[
            whole(base_query),
            whole(products),
            whole(factors),
            whole(gain),
            whole(key_new),
            whole(value_new),
            pl.BlockSpec((1, entries, HEAD), lambda i, place: (i, 0, 0)),
        ],
        out_specs=pl.BlockSpec((count, width), lambda i, place: (0, 0)),
        scratch_shapes=[
            pltpu.VMEM((count * width // HEAD, HEAD), jnp.float32),
            pltpu.VMEM((count * width // HEAD, HEAD), jnp.float32),
        ],
    )
    return pl.pallas_call(
        attend_kernel,
        out_shape=jax.ShapeDtypeStruct((count, width), jnp.bfloat16),
        grid_spec=spec,
        compiler_params=pltpu.CompilerParams(vmem_limit_bytes=VMEM_LIMIT),
        name="attend",
    )(place, base_query, products, factors, gain, key_new, value_new, cache)


def tensor_swap(values, bit):
    size = lax.axis_size("tensor")
    return lax.ppermute(values, "tensor", [(i, i ^ bit) for i in range(size)])


def body(
    token_ids,
    embed_table,
    norm_gain,
    query_gain,
    key_gain,
    base_query_weight,
    pair_weight,
    past_pairs,
    down_factor,
    up_factor,
    grad_down,
    grad_up,
    group_scale,
    learner_group,
):
    groups = lax.axis_size("dp")
    t = lax.axis_index("tensor")
    vocab_rows, width = embed_table.shape
    own_rank = down_factor.shape[0]
    pair_index = t * (width // HEAD) // (HEADS // KVH)
    place = jnp.stack([t, pair_index]).astype(jnp.int32)

    ids, slot = plan_tokens(token_ids, groups, vocab_rows)
    rounds = jnp.max(slot) // CAP + 1
    found = own_rows(ids, slot, 0, embed_table)

    own_down = lax.dynamic_slice_in_dim(grad_down[0], t * width, width, 1)
    half = width // 2

    def fold(rows):
        return rows.reshape(groups, own_rank * 2, half)

    sent = jnp.concatenate(
        [found, jnp.concatenate([fold(own_down), fold(grad_up[0])], axis=1)], axis=2
    )
    got = lax.all_to_all(sent, "dp", 0, 0, tiled=True)

    embedded = pick_rows(ids, slot, 0, vocab_rows, got[:, :, :width])

    def later_round(state):
        r, rows = state
        again = own_rows(ids, slot, r * CAP, embed_table)
        again = lax.all_to_all(again, "dp", 0, 0, tiled=True)
        return r + 1, rows + pick_rows(ids, slot, r * CAP, vocab_rows, again)

    _, embedded = lax.while_loop(lambda s: s[0] < rounds, later_round, (1, embedded))

    position = jnp.arange(groups, dtype=jnp.int32)
    chosen = learner_group[:, None] == position[None, :]
    weight = jnp.sum(jnp.where(chosen, group_scale[None, :], 0.0), axis=1)
    sums = jnp.sum(got[:, :, width:].astype(jnp.float32) * weight[:, None, None], axis=0)
    sums = sums.reshape(2 * own_rank, width)
    sum_down, sum_up = sums[:own_rank], sums[own_rank:]

    blocks = [embedded] + [tensor_swap(embedded, bit) for bit in (1, 2, 3)]
    own_factor = lax.dynamic_slice_in_dim(down_factor, t * width, width, 1)
    rows = jnp.concatenate([sums, own_factor, up_factor], axis=0)
    factors = lax.all_to_all(
        jnp.broadcast_to(rows[None], (groups,) + rows.shape), "dp", 0, 0, tiled=True
    )

    normed, products = project(place, blocks, norm_gain, factors)
    lanes = products.shape[1]
    count = products.shape[0]
    own_sum = sum_down.reshape(-1, lanes)
    other = tensor_swap(jnp.concatenate([products, own_sum], axis=0), 1)
    both = products + other[:count]
    other_sum = other[count:]
    is_odd = (t % 2) == 1
    pair_sum = jnp.stack(
        [jnp.where(is_odd, other_sum, own_sum), jnp.where(is_odd, own_sum, other_sum)]
    )
    far = tensor_swap(jnp.concatenate([both, pair_sum.reshape(-1, lanes)], axis=0), 2)
    products = both + far[:count]
    far_sum = far[count:].reshape(pair_sum.shape)
    is_high = t >= 2
    all_sum = jnp.concatenate(
        [jnp.where(is_high, far_sum, pair_sum), jnp.where(is_high, pair_sum, far_sum)]
    )
    full_down = all_sum.reshape(4, own_rank, width).transpose(1, 0, 2).reshape(own_rank, -1)

    query, key_new, value_new = base_products(
        place, normed, base_query_weight, pair_weight, key_gain
    )
    rows_here, context = past_pairs.shape[:2]
    cache = past_pairs.reshape(rows_here, context, KVH, 2, HEAD).transpose(0, 1, 3, 2, 4)
    cache = cache.reshape(rows_here, context * KVH * 2, HEAD)
    attended = attend(place, query, products, factors, query_gain, key_new, value_new, cache)

    clip_coef = 1.0 / jnp.maximum(jnp.sqrt(products[count - 8, 0]), 1.0)
    new_down = down_factor - RATE * clip_coef * full_down
    new_up = up_factor - RATE * clip_coef * sum_up
    return attended.reshape(STEPS, rows_here, width), new_down, new_up


def solution(mesh):
    in_specs = (
        P(),
        P("dp", "tensor"),
        P(),
        P(),
        P(),
        P(None, "tensor"),
        P(),
        P("dp", None, None, None),
        P("dp", None),
        P("dp", "tensor"),
        P("dp", None, None),
        P("dp", None, "tensor"),
        P(),
        P(),
    )
    out_specs = (P(None, "dp", "tensor"), P("dp", None), P("dp", "tensor"))
    return jax.shard_map(body, mesh=mesh, in_specs=in_specs, out_specs=out_specs, check_vma=False)
```

```python
import math

import jax
import jax.numpy as jnp
from jax import lax
from jax.experimental import pallas as pl
from jax.experimental.pallas import tpu as pltpu
from jax.sharding import PartitionSpec as P

D = 4096
HEAD = 128
HEADS = 32
KVH = 2
R = 64
STEPS = 4
HD = 4096
CAP = 8

TABLE_PARTS = 2

EPSILON = 1e-06
STEP_RATIO = 0.3
ADAPTER_SCALING = 1.0 / 1024.0
RATE = STEP_RATIO * math.sqrt(R * (D + HD))
MIB = 1024 * 1024


def split(values):
    high = values.astype(jnp.bfloat16)
    return high, (values - high.astype(jnp.float32)).astype(jnp.bfloat16)


def dot_nt(a, b):
    return lax.dot_general(a, b, (((1,), (1,)), ((), ())), preferred_element_type=jnp.float32)


def dot_nn(a, b):
    return lax.dot_general(a, b, (((1,), (0,)), ((), ())), preferred_element_type=jnp.float32)


def vmem():
    return pl.BlockSpec(memory_space=pltpu.VMEM)


def smem():
    return pl.BlockSpec(memory_space=pltpu.SMEM)


def whole(x):
    return pl.BlockSpec(x.shape, lambda *_: (0,) * len(x.shape))


def params(mib):
    return pltpu.CompilerParams(vmem_limit_bytes=mib * MIB)


def fold(down, up):
    half = down.shape[1] // 2
    rows = [x[i : i + 1, h * half : (h + 1) * half] for x in (down, up) for i in (0, 1) for h in (0, 1)]
    return jnp.concatenate(rows, axis=0)


def arrange_ids(tokens, groups):
    steps, rows = tokens.shape
    here = rows // groups
    row = lax.broadcasted_iota(jnp.int32, (groups, rows), 0)
    lane = lax.broadcasted_iota(jnp.int32, (groups, rows), 1)
    parts = []
    for s in range(steps):
        own = jnp.where(lane // here == row, jnp.broadcast_to(tokens[s : s + 1], lane.shape), 0)
        parts.append(own)
    wide = jnp.concatenate(parts, axis=1)
    pieces = jnp.concatenate([wide & 255, (wide >> 8) & 255, wide >> 16], axis=0)
    pieces = pieces.astype(jnp.float32).astype(jnp.bfloat16)
    source = lax.broadcasted_iota(jnp.int32, (steps * rows, 128), 0)
    target = lax.broadcasted_iota(jnp.int32, (steps * rows, 128), 1) % (steps * here)
    same = (source % here == target % here) & (source // rows == target // here)
    ids = dot_nn(pieces, jnp.where(same, 1.0, 0.0).astype(jnp.bfloat16)).astype(jnp.int32)
    return ids[:groups] + (ids[groups : 2 * groups] << 8) + (ids[2 * groups :] << 16)


def find_rows(place, first, ids, table, period, pick, places):
    groups, lanes = ids.shape
    vocab_rows = table.shape[0]
    lane = lax.broadcasted_iota(jnp.int32, ids.shape, 1) % period
    owner = ((ids.astype(jnp.float32) + 0.5) * (1.0 / vocab_rows)).astype(jnp.int32)
    lowest = owner * vocab_rows
    repeated = jnp.zeros(ids.shape, jnp.int32)
    for k in range(1, period):
        repeated = jnp.where((pltpu.roll(ids, k, 1) == ids) & (lane >= k), 1, repeated)
    distinct = jnp.where(repeated == 0, ids, -1)
    slot = jnp.zeros(ids.shape, jnp.int32)
    for k in range(1, period):
        other = pltpu.roll(distinct, k, 1)
        slot += jnp.where((other >= lowest) & (other < ids), 1, 0)
    rounds = jnp.max(slot) // CAP + 1
    slot -= first
    places[...] = jnp.where((slot >= 0) & (slot < CAP), owner * CAP + slot, -1)

    me = place[2]
    own = places[pl.ds(me, 1), :]
    rows = groups * CAP
    at = lax.broadcasted_iota(jnp.int32, (rows, lanes), 0)
    pick[...] = jnp.where(at == own, 1.0, 0.0).astype(jnp.bfloat16)[:, :period]

    local = jnp.where(owner == me, ids - lowest, -1)
    spread = (groups, CAP, lanes)
    local = jnp.broadcast_to(local[:, None, :], spread).reshape(rows, lanes)
    slot = jnp.broadcast_to(slot[:, None, :], spread).reshape(rows, lanes)
    wanted = lax.broadcasted_iota(jnp.int32, (rows, lanes), 0) % CAP
    chosen = jnp.max(jnp.where(slot == wanted, local, -1), axis=1, keepdims=True)
    return chosen, rounds


def one_hot(chosen, vocab_rows):
    at = lax.broadcasted_iota(jnp.int32, (chosen.shape[0], vocab_rows), 1)
    return jnp.where(at == chosen, 1.0, 0.0).astype(jnp.bfloat16)


def read_rows(hot, table):
    main = hot.shape[1] // 256 * 256
    found = dot_nn(hot[:, :main], table[:main, :])
    if main < hot.shape[1]:
        found += dot_nn(hot[:, main:], table[main:, :])
    return found.astype(jnp.bfloat16)


def send_kernel(
    place, tokens_at, table_at, grad_down_at, grad_up_at, down_at, up_at, sent, pick, rounds,
    tokens, table, grad_down, grad_up, down, up, places, sems,
):
    groups = sent.shape[0] // CAP
    vocab_rows, width = table.shape
    half = width // 2
    ranks = grad_up.shape[1]
    columns = pl.ds(pl.multiple_of(place[0] * width, width), width)
    copies = [
        pltpu.make_async_copy(source, target, sems.at[i])
        for i, (source, target) in enumerate(
            (
                (tokens_at, tokens),
                (grad_down_at.at[:, :, columns], grad_down),
                (grad_up_at, grad_up),
                (down_at, down),
                (up_at, up),
            )
        )
    ]
    span = width // TABLE_PARTS
    spans = [slice(i * span, (i + 1) * span) for i in range(TABLE_PARTS)]
    copies += [
        pltpu.make_async_copy(table_at.at[:, at], table.at[:, at], sems.at[5 + i])
        for i, at in enumerate(spans)
    ]
    for copy in copies:
        copy.start()
    copies[0].wait()
    ids = arrange_ids(tokens[...], groups)
    chosen, count = find_rows(place, 0, ids, table, pick.shape[1], pick, places)
    rounds[0] = count
    for copy in copies[1:5]:
        copy.wait()

    grads = jnp.concatenate([grad_down[0], grad_up[0]], axis=0)
    row = lax.broadcasted_iota(jnp.int32, (groups * 8, 2 * ranks), 0)
    source = lax.broadcasted_iota(jnp.int32, (groups * 8, 2 * ranks), 1)
    wanted = row // 4 % 2 * ranks + row // 8 * 2 + row // 2 % 2
    moved = jnp.zeros((groups * 8, half), jnp.float32)
    for h in (0, 1):
        taken = jnp.where((source == wanted) & (row % 2 == h), 1.0, 0.0).astype(jnp.bfloat16)
        moved += dot_nn(taken, grads[:, h * half : (h + 1) * half])
    sent[:, width : width + half] = moved.astype(jnp.bfloat16)
    for i, part in enumerate(split(fold(down[:, columns], up[...]))):
        part = jnp.broadcast_to(part[None], (groups, 8, half)).reshape(groups * 8, half)
        sent[:, width + (1 + i) * half : width + (2 + i) * half] = part

    hot = one_hot(chosen, vocab_rows)
    for i, at in enumerate(spans):
        copies[5 + i].wait()
        sent[:, at] = read_rows(hot, table.at[:, at])


def send(place, tokens, table, grad_down, grad_up, down, up, groups):
    width = table.shape[1]
    count = tokens.size // groups
    anywhere = pl.BlockSpec(memory_space=pl.ANY)
    return pl.pallas_call(
        send_kernel,
        out_shape=(
            jax.ShapeDtypeStruct((groups * CAP, width * 5 // 2), jnp.bfloat16),
            jax.ShapeDtypeStruct((groups * CAP, count), jnp.bfloat16),
            jax.ShapeDtypeStruct((1,), jnp.int32),
        ),
        in_specs=[smem()] + [anywhere] * 6,
        out_specs=(vmem(), vmem(), smem()),
        scratch_shapes=[
            pltpu.VMEM(tokens.shape, jnp.int32),
            pltpu.VMEM(table.shape, jnp.bfloat16),
            pltpu.VMEM(grad_up.shape, jnp.bfloat16),
            pltpu.VMEM(grad_up.shape, jnp.bfloat16),
            pltpu.VMEM(down.shape, jnp.float32),
            pltpu.VMEM(up.shape, jnp.float32),
            pltpu.VMEM((groups, 128), jnp.int32),
            pltpu.SemaphoreType.DMA((5 + TABLE_PARTS,)),
        ],
        compiler_params=params(56),
        name="send",
    )(place, tokens, table, grad_down, grad_up, down, up)


def again_kernel(place, first, tokens, table, sent, pick, places):
    groups = sent.shape[0] // CAP
    ids = arrange_ids(tokens[...], groups)
    chosen, _ = find_rows(place, first[0], ids, table, pick.shape[1], pick, places)
    sent[...] = read_rows(one_hot(chosen, table.shape[0]), table)


def again(place, first, tokens, table, groups):
    return pl.pallas_call(
        again_kernel,
        out_shape=(
            jax.ShapeDtypeStruct((groups * CAP, table.shape[1]), jnp.bfloat16),
            jax.ShapeDtypeStruct((groups * CAP, tokens.size // groups), jnp.bfloat16),
        ),
        in_specs=[smem(), smem(), vmem(), vmem()],
        out_specs=(vmem(), vmem()),
        scratch_shapes=[pltpu.VMEM((groups, 128), jnp.int32)],
        compiler_params=params(20),
        name="again",
    )(place, first, tokens, table)


def gather_kernel(scale, learner, got, pick, extra, block, own_sum, sent):
    groups = got.shape[0]
    count, width = extra.shape
    half = width // 2
    total = jnp.zeros((8, half), jnp.float32)
    for learn in range(groups):
        weight = scale[learner[learn]]
        total += got[learn, :, width : width + half].astype(jnp.float32) * weight
    own_sum[...] = total
    sent[...] = jnp.broadcast_to(total[None], sent.shape)
    rows = got[:, :, :width].reshape(groups * CAP, width)
    found = lax.dot_general(
        pick[...], rows, (((0,), (0,)), ((), ())), preferred_element_type=jnp.float32
    )
    block[:count, :] = found.astype(jnp.bfloat16) + extra[...]
    down = jnp.concatenate(
        [jnp.concatenate([total[2 * i : 2 * i + 1], total[2 * i + 1 : 2 * i + 2]], 1) for i in (0, 1)], 0
    )
    first, _ = split(down)
    second, third = split(down - first.astype(jnp.float32))
    rows = [first, second, third, jnp.zeros((10, width), jnp.bfloat16)]
    block[count:, :] = jnp.concatenate([r.astype(jnp.float32) for r in rows], 0).astype(jnp.bfloat16)


def gather(scale, learner, got, pick, extra):
    groups = got.shape[0]
    count, width = extra.shape
    return pl.pallas_call(
        gather_kernel,
        out_shape=(
            jax.ShapeDtypeStruct((count + 16, width), jnp.bfloat16),
            jax.ShapeDtypeStruct((8, width // 2), jnp.float32),
            jax.ShapeDtypeStruct((groups, 8, width // 2), jnp.float32),
        ),
        in_specs=[smem(), smem(), vmem(), vmem(), vmem()],
        out_specs=(vmem(), vmem(), vmem()),
        compiler_params=params(8),
        name="gather",
    )(scale, learner, got, pick, extra)


def stage_kernel(place, cache_at, keys_at, values_at, cache, keys, values, wide, sems):
    rows, _, count = keys.shape
    copies = [pltpu.make_async_copy(cache_at.at[i], cache.at[i], sems.at[i]) for i in range(rows)]
    for copy in copies:
        copy.start()
    back = []
    for i in range(rows):
        copies[i].wait()
        wide[...] = cache[i].astype(jnp.float32)
        keys[i] = wide[pl.ds(place[1], count, stride=4), :].T.astype(jnp.bfloat16)
        values[i] = wide[pl.ds(place[1] + 2, count, stride=4), :].astype(jnp.bfloat16)
        back.append(pltpu.make_async_copy(keys.at[i], keys_at.at[i], sems.at[rows + 2 * i]))
        back.append(pltpu.make_async_copy(values.at[i], values_at.at[i], sems.at[rows + 2 * i + 1]))
        back[-2].start()
        back[-1].start()
    for copy in back:
        copy.wait()


def stage(place, cache, after):
    rows, entries, _ = cache.shape
    place, _ = lax.optimization_barrier((place, after))
    anywhere = pl.BlockSpec(memory_space=pl.ANY)
    keys = jax.ShapeDtypeStruct((rows, HEAD, entries // 4), jnp.bfloat16)
    values = jax.ShapeDtypeStruct((rows, entries // 4, HEAD), jnp.bfloat16)
    return pl.pallas_call(
        stage_kernel,
        out_shape=[keys, values],
        in_specs=[smem(), anywhere],
        out_specs=[anywhere] * 2,
        scratch_shapes=[
            pltpu.VMEM(cache.shape, jnp.bfloat16),
            pltpu.VMEM(keys.shape, jnp.bfloat16),
            pltpu.VMEM(values.shape, jnp.bfloat16),
            pltpu.VMEM((entries, HEAD), jnp.float32),
            pltpu.SemaphoreType.DMA((3 * rows,)),
        ],
        compiler_params=params(58),
        cost_estimate=pl.CostEstimate(flops=0, bytes_accessed=2**23, transcendentals=0),
        name="stage",
    )(place, cache)


def pair_kernel(place, normed, gain, pair_at, key_new, value_new, pair, sem):
    copy = pltpu.make_async_copy(pair_at.at[place[1]], pair, sem)
    copy.start()
    copy.wait()
    pairs = dot_nn(normed[...], pair[...])
    keys = pairs[:, :HEAD]
    scale = lax.rsqrt(jnp.mean(keys * keys, axis=1, keepdims=True) + EPSILON)
    key_new[...] = (keys * scale * gain[...]).astype(jnp.bfloat16)
    value_new[...] = pairs[:, HEAD:].astype(jnp.bfloat16)


def pair_products(place, normed, gain, pair):
    fresh = jax.ShapeDtypeStruct((normed.shape[0], HEAD), jnp.bfloat16)
    return pl.pallas_call(
        pair_kernel,
        out_shape=(fresh, fresh),
        in_specs=[smem(), vmem(), vmem(), pl.BlockSpec(memory_space=pl.ANY)],
        out_specs=(vmem(), vmem()),
        scratch_shapes=[
            pltpu.VMEM(pair.shape[1:], jnp.bfloat16),
            pltpu.SemaphoreType.DMA(()),
        ],
        compiler_params=params(58),
        cost_estimate=pl.CostEstimate(flops=0, bytes_accessed=2**23, transcendentals=0),
        name="pair_products",
    )(place, normed, gain.reshape(1, -1), pair)


def fetch_kernel(place, keys_at, values_at, keys, values, sems):
    copies = [
        pltpu.make_async_copy(keys_at, keys, sems.at[0]),
        pltpu.make_async_copy(values_at, values, sems.at[1]),
    ]
    for copy in copies:
        copy.start()
    for copy in copies:
        copy.wait()


def fetch(place, keys, values, after):
    place, _ = lax.optimization_barrier((place, after))
    return pl.pallas_call(
        fetch_kernel,
        out_shape=[jax.ShapeDtypeStruct(x.shape, x.dtype) for x in (keys, values)],
        in_specs=[smem()] + [pl.BlockSpec(memory_space=pl.ANY)] * 2,
        out_specs=[vmem(), vmem()],
        scratch_shapes=[pltpu.SemaphoreType.DMA((2,))],
        compiler_params=params(1),
        cost_estimate=pl.CostEstimate(flops=0, bytes_accessed=2**22, transcendentals=0),
        name="fetch",
    )(place, keys, values)


def norm_kernel(place, e0, e1, e2, e3, gain, normed, own):
    t = place[0]
    count, width = own.shape
    blocks = [e[:count, :].astype(jnp.float32) for e in (e0, e1, e2, e3)]
    square = sum(jnp.sum(b * b, axis=1, keepdims=True) for b in blocks)
    scale = lax.rsqrt(square / D + EPSILON)
    for k, block in enumerate(blocks):
        columns = pl.ds(pl.multiple_of((t ^ k) * width, width), width)
        value = (block * scale * gain[:, columns]).astype(jnp.bfloat16)
        normed[:, columns] = value
        if k == 0:
            own[...] = value


def norm(place, blocks, gain, count):
    width = blocks[0].shape[1]
    return pl.pallas_call(
        norm_kernel,
        out_shape=(
            jax.ShapeDtypeStruct((count, 4 * width), jnp.bfloat16),
            jax.ShapeDtypeStruct((count, width), jnp.bfloat16),
        ),
        in_specs=[smem()] + [vmem()] * 5,
        out_specs=(vmem(), vmem()),
        compiler_params=params(8),
        name="norm",
    )(place, *blocks, gain.reshape(1, -1))


def old_factors(got, half):
    return got[:, :, 3 * half : 4 * half], got[:, :, 4 * half :]


def products_kernel(own, sums, got, out):
    count = own.shape[0]
    half = sums.shape[2]

    def combine(parts):
        left = sum(dot_nt(own[:, :half], p) for p in parts)
        right = sum(dot_nt(own[:, half:], p) for p in parts)
        lane = lax.broadcasted_iota(jnp.int32, left.shape, 1)
        mixed = jnp.where(lane % 2 == 0, left, right)
        mixed = mixed + pltpu.roll(mixed, mixed.shape[1] - 1, 1)
        return jnp.where((lane % 8 == 0) | (lane % 8 == 2), mixed, 0.0)

    rows = sums[...].reshape(-1, half)
    high, low = old_factors(got, half)
    old = combine([high.reshape(-1, half), low.reshape(-1, half)])
    new = combine(split(rows))
    out[:count, :] = new + pltpu.roll(old, 1, 1)
    out[count:, :] = jnp.full((8, rows.shape[0]), jnp.sum(rows * rows), jnp.float32)


def products(own, sums, got):
    count = own.shape[0]
    return pl.pallas_call(
        products_kernel,
        out_shape=jax.ShapeDtypeStruct((count + 8, sums.shape[0] * 8), jnp.float32),
        in_specs=[vmem()] * 3,
        out_specs=vmem(),
        compiler_params=params(8),
        name="products",
    )(own, sums, got)


def attend_kernel(
    place, base_query, p0, p1, p2, p3, sums, got, gain, key_new, value_new, s0, s1, s2,
    s3, own_sum, old_down, old_up, keys, values, out, new_down, new_up, queries, results,
):
    t = place[0]
    rows_here = keys.shape[0]
    count, width = base_query.shape
    heads = width // HEAD
    steps = count // rows_here
    per_row = steps * heads
    half = width // 2

    both = (p0[...] + p1[...]) + (p2[...] + p3[...])
    product = both[:count, :]
    overall = both[count : count + 1, :]
    clip = RATE * (1.0 / jnp.maximum(jnp.sqrt(overall), 1.0))
    lanes = product.shape[1]
    lane = lax.broadcasted_iota(jnp.int32, product.shape, 1) % 8
    updated = pltpu.roll(product, lanes - 1, 1) - clip * product
    updated = jnp.where((lane == 0) | (lane == 2), updated, 0.0)
    clip = clip[:, :1]
    high, low = old_factors(got, half)
    old = high.astype(jnp.float32) + low.astype(jnp.float32)
    rows = (old - clip[None] * sums[...]).reshape(-1, half)
    row_high, row_low = split(rows)
    for h in (0, 1):
        left_high, left_low = split(pltpu.roll(updated, 4 + h, 1))
        change = dot_nn(left_high, row_high) + dot_nn(left_low, row_high)
        change += dot_nn(left_high, row_low)
        query = base_query[:, h * half : (h + 1) * half] + ADAPTER_SCALING * change
        for j in range(heads // 2):
            part = query[:, j * HEAD : (j + 1) * HEAD]
            scale = lax.rsqrt(jnp.mean(part * part, axis=1, keepdims=True) + EPSILON)
            part = (part * scale * gain[...]).astype(jnp.bfloat16).astype(jnp.float32)
            for s in range(steps):
                at = s * heads + h * (heads // 2) + j
                queries[pl.ds(at, rows_here, stride=per_row), :] = part[
                    s * rows_here : (s + 1) * rows_here
                ]

    inverse = 1.0 / math.sqrt(HEAD)
    new_lane = lax.broadcasted_iota(jnp.int32, (per_row, count), 1)
    step = lax.broadcasted_iota(jnp.int32, (per_row, count), 0) // heads
    seen = new_lane // rows_here <= step
    query = queries[...].astype(jnp.bfloat16)
    own = [slice(row * per_row, (row + 1) * per_row) for row in range(rows_here)]
    fresh = dot_nt(query, key_new[...]) * inverse
    old, new = [], []
    for row in range(rows_here):
        old.append(dot_nn(query[own[row]], keys[row]) * inverse)
        new.append(jnp.where((new_lane % rows_here == row) & seen, fresh[own[row]], -jnp.inf))
    for row in range(rows_here):
        top = jnp.maximum(
            jnp.max(old[row], axis=1, keepdims=True), jnp.max(new[row], axis=1, keepdims=True)
        )
        old[row], new[row] = jnp.exp(old[row] - top), jnp.exp(new[row] - top)
    for row in range(rows_here):
        total = jnp.sum(old[row], axis=1, keepdims=True) + jnp.sum(new[row], axis=1, keepdims=True)
        share = 1.0 / total
        old[row] = (old[row] * share).astype(jnp.bfloat16)
        new[row] = (new[row] * share).astype(jnp.bfloat16)
    for row in range(rows_here):
        results[own[row], :] = dot_nn(old[row], values[row]) + dot_nn(new[row], value_new[...])

    for h in range(heads):
        parts = [results[pl.ds(s * heads + h, rows_here, stride=per_row), :] for s in range(steps)]
        out[:, h * HEAD : (h + 1) * HEAD] = jnp.concatenate(parts, 0).astype(jnp.bfloat16)

    for k, block in enumerate((s0, s1, s2, s3)):
        columns = pl.ds(pl.multiple_of((t ^ k) * width, width), width)
        part = block[count : count + 16, :].astype(jnp.float32)
        summed = (part[0:2] + part[2:4]) + part[4:6]
        new_down[:, columns] = old_down[:, columns] - clip * summed
    up = own_sum[...]
    for i in (0, 1):
        for h in (0, 1):
            columns = slice(h * half, (h + 1) * half)
            value = up[4 + 2 * i + h : 5 + 2 * i + h, :]
            new_up[i : i + 1, columns] = old_up[i : i + 1, columns] - clip * value


def attend(place, *arrays):
    base_query = arrays[0]
    count, width = base_query.shape
    old_down, old_up = arrays[-4:-2]
    return pl.pallas_call(
        attend_kernel,
        out_shape=(
            jax.ShapeDtypeStruct((count, width), jnp.bfloat16),
            jax.ShapeDtypeStruct(old_down.shape, jnp.float32),
            jax.ShapeDtypeStruct(old_up.shape, jnp.float32),
        ),
        in_specs=[smem()] + [vmem()] * len(arrays),
        out_specs=(vmem(), vmem(), vmem()),
        scratch_shapes=[
            pltpu.VMEM((count * width // HEAD, HEAD), jnp.float32),
            pltpu.VMEM((count * width // HEAD, HEAD), jnp.float32),
        ],
        compiler_params=params(16),
        name="attend",
    )(place, *arrays)


def tensor_swap(values, bit):
    size = lax.axis_size("tensor")
    return lax.ppermute(values, "tensor", [(i, i ^ bit) for i in range(size)])


def body(
    token_ids,
    embed_table,
    norm_gain,
    query_gain,
    key_gain,
    base_query_weight,
    pair_weight,
    past_pairs,
    down_factor,
    up_factor,
    grad_down,
    grad_up,
    group_scale,
    learner_group,
):
    groups = lax.axis_size("dp")
    t = lax.axis_index("tensor")
    me = lax.axis_index("dp")
    width = embed_table.shape[1]
    half = width // 2
    pair_index = t * (width // HEAD) // (HEADS // KVH)
    place = jnp.stack([t, pair_index, me]).astype(jnp.int32)
    rows_here, context = past_pairs.shape[:2]
    steps = token_ids.shape[0]
    count = steps * rows_here

    sent, pick, rounds = send(
        place, token_ids, embed_table, grad_down, grad_up, down_factor, up_factor, groups
    )
    got = lax.all_to_all(sent.reshape(groups, CAP, -1), "dp", 0, 0, tiled=True)

    def later_round(state):
        r, rows = state
        sent, pick = again(place, (r * CAP).reshape(1), token_ids, embed_table, groups)
        back = lax.all_to_all(sent.reshape(groups, CAP, -1), "dp", 0, 0, tiled=True)
        found = lax.dot_general(
            pick,
            back.reshape(groups * CAP, width),
            (((0,), (0,)), ((), ())),
            preferred_element_type=jnp.float32,
        )
        return r + 1, rows + found.astype(jnp.bfloat16)

    _, extra = lax.while_loop(
        lambda s: s[0] < rounds[0],
        later_round,
        (jnp.int32(1), jnp.zeros((count, width), jnp.bfloat16)),
    )
    cache = past_pairs.reshape(rows_here, context, KVH, 2, HEAD).transpose(0, 1, 3, 2, 4)
    cache = cache.reshape(rows_here, context * KVH * 2, HEAD)
    keys, values = stage(place, cache, pick)
    pick, keys, values = lax.optimization_barrier((pick, keys, values))
    block, own_sum, sums = gather(group_scale, learner_group, got, pick, extra)
    sums = lax.all_to_all(sums, "dp", 0, 0, tiled=True)

    blocks = [block] + [tensor_swap(block, bit) for bit in (1, 2, 3)]
    normed, own = norm(place, blocks, norm_gain, count)

    key_new, value_new = pair_products(place, normed, key_gain, pair_weight)
    query = jnp.dot(normed, base_query_weight, preferred_element_type=jnp.float32)
    own, query, key_new = lax.optimization_barrier((own, query, key_new))

    part = products(own, sums, got)
    keys, values = fetch(place, keys, values, part)
    parts = [part] + [tensor_swap(part, bit) for bit in (1, 2, 3)]
    attended, new_down, new_up = attend(
        place, query, *parts, sums, got, query_gain.reshape(1, -1), key_new, value_new,
        *blocks, own_sum, down_factor, up_factor, keys, values,
    )
    return attended.reshape(steps, rows_here, width), new_down, new_up


def solution(mesh):
    in_specs = (
        P(),
        P("dp", "tensor"),
        P(),
        P(),
        P(),
        P(None, "tensor"),
        P(),
        P("dp", None, None, None),
        P("dp", None),
        P("dp", "tensor"),
        P("dp", None, None),
        P("dp", None, "tensor"),
        P(),
        P(),
    )
    out_specs = (P(None, "dp", "tensor"), P("dp", None), P("dp", "tensor"))
    return jax.shard_map(body, mesh=mesh, in_specs=in_specs, out_specs=out_specs, check_vma=False)
```

```python
import math

import jax
import jax.numpy as jnp
from jax import lax
from jax.experimental import pallas as pl
from jax.experimental.pallas import tpu as pltpu
from jax.sharding import PartitionSpec as P

D = 4096
HEAD = 128
HEADS = 32
KVH = 2
R = 64
STEPS = 4
HD = 4096
CAP = 8

TABLE_PARTS = 2

EPSILON = 1e-06
STEP_RATIO = 0.3
ADAPTER_SCALING = 1.0 / 1024.0
RATE = STEP_RATIO * math.sqrt(R * (D + HD))
MIB = 1024 * 1024


def split(values):
    high = values.astype(jnp.bfloat16)
    return high, (values - high.astype(jnp.float32)).astype(jnp.bfloat16)


def dot_nt(a, b):
    return lax.dot_general(a, b, (((1,), (1,)), ((), ())), preferred_element_type=jnp.float32)


def dot_nn(a, b):
    return lax.dot_general(a, b, (((1,), (0,)), ((), ())), preferred_element_type=jnp.float32)


def vmem():
    return pl.BlockSpec(memory_space=pltpu.VMEM)


def smem():
    return pl.BlockSpec(memory_space=pltpu.SMEM)


def whole(x):
    return pl.BlockSpec(x.shape, lambda *_: (0,) * len(x.shape))


def params(mib):
    return pltpu.CompilerParams(vmem_limit_bytes=mib * MIB)


def fold(down, up):
    half = down.shape[1] // 2
    rows = [x[i : i + 1, h * half : (h + 1) * half] for x in (down, up) for i in (0, 1) for h in (0, 1)]
    return jnp.concatenate(rows, axis=0)


def arrange_ids(tokens, groups):
    steps, rows = tokens.shape
    here = rows // groups
    row = lax.broadcasted_iota(jnp.int32, (groups, rows), 0)
    lane = lax.broadcasted_iota(jnp.int32, (groups, rows), 1)
    parts = []
    for s in range(steps):
        own = jnp.where(lane // here == row, jnp.broadcast_to(tokens[s : s + 1], lane.shape), 0)
        parts.append(own)
    wide = jnp.concatenate(parts, axis=1)
    pieces = jnp.concatenate([wide & 255, (wide >> 8) & 255, wide >> 16], axis=0)
    pieces = pieces.astype(jnp.float32).astype(jnp.bfloat16)
    source = lax.broadcasted_iota(jnp.int32, (steps * rows, 128), 0)
    target = lax.broadcasted_iota(jnp.int32, (steps * rows, 128), 1) % (steps * here)
    same = (source % here == target % here) & (source // rows == target // here)
    ids = dot_nn(pieces, jnp.where(same, 1.0, 0.0).astype(jnp.bfloat16)).astype(jnp.int32)
    return ids[:groups] + (ids[groups : 2 * groups] << 8) + (ids[2 * groups :] << 16)


def find_rows(place, first, ids, table, period, pick, places):
    groups, lanes = ids.shape
    vocab_rows = table.shape[0]
    lane = lax.broadcasted_iota(jnp.int32, ids.shape, 1) % period
    owner = ((ids.astype(jnp.float32) + 0.5) * (1.0 / vocab_rows)).astype(jnp.int32)
    lowest = owner * vocab_rows
    repeated = jnp.zeros(ids.shape, jnp.int32)
    for k in range(1, period):
        repeated = jnp.where((pltpu.roll(ids, k, 1) == ids) & (lane >= k), 1, repeated)
    distinct = jnp.where(repeated == 0, ids, -1)
    slot = jnp.zeros(ids.shape, jnp.int32)
    for k in range(1, period):
        other = pltpu.roll(distinct, k, 1)
        slot += jnp.where((other >= lowest) & (other < ids), 1, 0)
    rounds = jnp.max(slot) // CAP + 1
    slot -= first
    places[...] = jnp.where((slot >= 0) & (slot < CAP), owner * CAP + slot, -1)

    me = place[2]
    own = places[pl.ds(me, 1), :]
    rows = groups * CAP
    at = lax.broadcasted_iota(jnp.int32, (rows, lanes), 0)
    pick[...] = jnp.where(at == own, 1.0, 0.0).astype(jnp.bfloat16)[:, :period]

    local = jnp.where(owner == me, ids - lowest, -1)
    spread = (groups, CAP, lanes)
    local = jnp.broadcast_to(local[:, None, :], spread).reshape(rows, lanes)
    slot = jnp.broadcast_to(slot[:, None, :], spread).reshape(rows, lanes)
    wanted = lax.broadcasted_iota(jnp.int32, (rows, lanes), 0) % CAP
    chosen = jnp.max(jnp.where(slot == wanted, local, -1), axis=1, keepdims=True)
    return chosen, rounds


def one_hot(chosen, vocab_rows):
    at = lax.broadcasted_iota(jnp.int32, (chosen.shape[0], vocab_rows), 1)
    return jnp.where(at == chosen, 1.0, 0.0).astype(jnp.bfloat16)


def read_rows(hot, table):
    main = hot.shape[1] // 256 * 256
    found = dot_nn(hot[:, :main], table[:main, :])
    if main < hot.shape[1]:
        found += dot_nn(hot[:, main:], table[main:, :])
    return found.astype(jnp.bfloat16)


def send_kernel(
    place, tokens_at, table_at, grad_down_at, grad_up_at, down_at, up_at, sent, pick, rounds,
    tokens, table, grad_down, grad_up, down, up, places, sems,
):
    groups = sent.shape[0] // CAP
    vocab_rows, width = table.shape
    half = width // 2
    ranks = grad_up.shape[1]
    columns = pl.ds(pl.multiple_of(place[0] * width, width), width)
    copies = [
        pltpu.make_async_copy(source, target, sems.at[i])
        for i, (source, target) in enumerate(
            (
                (tokens_at, tokens),
                (grad_down_at.at[:, :, columns], grad_down),
                (grad_up_at, grad_up),
                (down_at, down),
                (up_at, up),
            )
        )
    ]
    span = width // TABLE_PARTS
    spans = [slice(i * span, (i + 1) * span) for i in range(TABLE_PARTS)]
    copies += [
        pltpu.make_async_copy(table_at.at[:, at], table.at[:, at], sems.at[5 + i])
        for i, at in enumerate(spans)
    ]
    for copy in copies:
        copy.start()
    copies[0].wait()
    ids = arrange_ids(tokens[...], groups)
    chosen, count = find_rows(place, 0, ids, table, pick.shape[1], pick, places)
    rounds[0] = count
    for copy in copies[1:5]:
        copy.wait()

    grads = jnp.concatenate([grad_down[0], grad_up[0]], axis=0)
    row = lax.broadcasted_iota(jnp.int32, (groups * 8, 2 * ranks), 0)
    source = lax.broadcasted_iota(jnp.int32, (groups * 8, 2 * ranks), 1)
    wanted = row // 4 % 2 * ranks + row // 8 * 2 + row // 2 % 2
    moved = jnp.zeros((groups * 8, half), jnp.float32)
    for h in (0, 1):
        taken = jnp.where((source == wanted) & (row % 2 == h), 1.0, 0.0).astype(jnp.bfloat16)
        moved += dot_nn(taken, grads[:, h * half : (h + 1) * half])
    sent[:, width : width + half] = moved.astype(jnp.bfloat16)
    rows = fold(down[:, columns], up[...]).astype(jnp.bfloat16)
    sent[:, width + half :] = jnp.broadcast_to(rows[None], (groups, 8, half)).reshape(-1, half)

    hot = one_hot(chosen, vocab_rows)
    for i, at in enumerate(spans):
        copies[5 + i].wait()
        sent[:, at] = read_rows(hot, table.at[:, at])


def send(place, tokens, table, grad_down, grad_up, down, up, groups):
    width = table.shape[1]
    count = tokens.size // groups
    anywhere = pl.BlockSpec(memory_space=pl.ANY)
    return pl.pallas_call(
        send_kernel,
        out_shape=(
            jax.ShapeDtypeStruct((groups * CAP, width * 2), jnp.bfloat16),
            jax.ShapeDtypeStruct((groups * CAP, count), jnp.bfloat16),
            jax.ShapeDtypeStruct((1,), jnp.int32),
        ),
        in_specs=[smem()] + [anywhere] * 6,
        out_specs=(vmem(), vmem(), smem()),
        scratch_shapes=[
            pltpu.VMEM(tokens.shape, jnp.int32),
            pltpu.VMEM(table.shape, jnp.bfloat16),
            pltpu.VMEM(grad_up.shape, jnp.bfloat16),
            pltpu.VMEM(grad_up.shape, jnp.bfloat16),
            pltpu.VMEM(down.shape, jnp.float32),
            pltpu.VMEM(up.shape, jnp.float32),
            pltpu.VMEM((groups, 128), jnp.int32),
            pltpu.SemaphoreType.DMA((5 + TABLE_PARTS,)),
        ],
        compiler_params=params(56),
        name="send",
    )(place, tokens, table, grad_down, grad_up, down, up)


def again_kernel(place, first, tokens, table, sent, pick, places):
    groups = sent.shape[0] // CAP
    ids = arrange_ids(tokens[...], groups)
    chosen, _ = find_rows(place, first[0], ids, table, pick.shape[1], pick, places)
    sent[...] = read_rows(one_hot(chosen, table.shape[0]), table)


def again(place, first, tokens, table, groups):
    return pl.pallas_call(
        again_kernel,
        out_shape=(
            jax.ShapeDtypeStruct((groups * CAP, table.shape[1]), jnp.bfloat16),
            jax.ShapeDtypeStruct((groups * CAP, tokens.size // groups), jnp.bfloat16),
        ),
        in_specs=[smem(), smem(), vmem(), vmem()],
        out_specs=(vmem(), vmem()),
        scratch_shapes=[pltpu.VMEM((groups, 128), jnp.int32)],
        compiler_params=params(20),
        name="again",
    )(place, first, tokens, table)


def gather_kernel(scale, learner, got, pick, extra, block, own_sum, sent):
    groups = got.shape[0]
    count, width = extra.shape
    half = width // 2
    total = jnp.zeros((8, half), jnp.float32)
    for learn in range(groups):
        weight = scale[learner[learn]]
        total += got[learn, :, width : width + half].astype(jnp.float32) * weight
    own_sum[...] = total
    sent[...] = jnp.broadcast_to(total[None], sent.shape)
    rows = got[:, :, :width].reshape(groups * CAP, width)
    found = lax.dot_general(
        pick[...], rows, (((0,), (0,)), ((), ())), preferred_element_type=jnp.float32
    )
    block[:count, :] = found.astype(jnp.bfloat16) + extra[...]
    down = jnp.concatenate(
        [jnp.concatenate([total[2 * i : 2 * i + 1], total[2 * i + 1 : 2 * i + 2]], 1) for i in (0, 1)], 0
    )
    first, _ = split(down)
    second, third = split(down - first.astype(jnp.float32))
    rows = [first, second, third, jnp.zeros((10, width), jnp.bfloat16)]
    block[count:, :] = jnp.concatenate([r.astype(jnp.float32) for r in rows], 0).astype(jnp.bfloat16)


def gather(scale, learner, got, pick, extra):
    groups = got.shape[0]
    count, width = extra.shape
    return pl.pallas_call(
        gather_kernel,
        out_shape=(
            jax.ShapeDtypeStruct((count + 16, width), jnp.bfloat16),
            jax.ShapeDtypeStruct((8, width // 2), jnp.float32),
            jax.ShapeDtypeStruct((groups, 8, width // 2), jnp.float32),
        ),
        in_specs=[smem(), smem(), vmem(), vmem(), vmem()],
        out_specs=(vmem(), vmem(), vmem()),
        compiler_params=params(8),
        name="gather",
    )(scale, learner, got, pick, extra)


def stage_kernel(place, cache_at, keys_at, values_at, cache, keys, values, wide, sems):
    rows, _, count = keys.shape
    copies = [pltpu.make_async_copy(cache_at.at[i], cache.at[i], sems.at[i]) for i in range(rows)]
    for copy in copies:
        copy.start()
    back = []
    for i in range(rows):
        copies[i].wait()
        wide[...] = cache[i].astype(jnp.float32)
        keys[i] = wide[pl.ds(place[1], count, stride=4), :].T.astype(jnp.bfloat16)
        values[i] = wide[pl.ds(place[1] + 2, count, stride=4), :].astype(jnp.bfloat16)
        back.append(pltpu.make_async_copy(keys.at[i], keys_at.at[i], sems.at[rows + 2 * i]))
        back.append(pltpu.make_async_copy(values.at[i], values_at.at[i], sems.at[rows + 2 * i + 1]))
        back[-2].start()
        back[-1].start()
    for copy in back:
        copy.wait()


def stage(place, cache, after):
    rows, entries, _ = cache.shape
    place, _ = lax.optimization_barrier((place, after))
    anywhere = pl.BlockSpec(memory_space=pl.ANY)
    keys = jax.ShapeDtypeStruct((rows, HEAD, entries // 4), jnp.bfloat16)
    values = jax.ShapeDtypeStruct((rows, entries // 4, HEAD), jnp.bfloat16)
    return pl.pallas_call(
        stage_kernel,
        out_shape=[keys, values],
        in_specs=[smem(), anywhere],
        out_specs=[anywhere] * 2,
        scratch_shapes=[
            pltpu.VMEM(cache.shape, jnp.bfloat16),
            pltpu.VMEM(keys.shape, jnp.bfloat16),
            pltpu.VMEM(values.shape, jnp.bfloat16),
            pltpu.VMEM((entries, HEAD), jnp.float32),
            pltpu.SemaphoreType.DMA((3 * rows,)),
        ],
        compiler_params=params(58),
        cost_estimate=pl.CostEstimate(flops=0, bytes_accessed=2**23, transcendentals=0),
        name="stage",
    )(place, cache)


def pair_kernel(place, normed, gain, pair_at, key_new, value_new, pair, sem):
    copy = pltpu.make_async_copy(pair_at.at[place[1]], pair, sem)
    copy.start()
    copy.wait()
    pairs = dot_nn(normed[...], pair[...])
    keys = pairs[:, :HEAD]
    scale = lax.rsqrt(jnp.mean(keys * keys, axis=1, keepdims=True) + EPSILON)
    key_new[...] = (keys * scale * gain[...]).astype(jnp.bfloat16)
    value_new[...] = pairs[:, HEAD:].astype(jnp.bfloat16)


def pair_products(place, normed, gain, pair):
    fresh = jax.ShapeDtypeStruct((normed.shape[0], HEAD), jnp.bfloat16)
    return pl.pallas_call(
        pair_kernel,
        out_shape=(fresh, fresh),
        in_specs=[smem(), vmem(), vmem(), pl.BlockSpec(memory_space=pl.ANY)],
        out_specs=(vmem(), vmem()),
        scratch_shapes=[
            pltpu.VMEM(pair.shape[1:], jnp.bfloat16),
            pltpu.SemaphoreType.DMA(()),
        ],
        compiler_params=params(58),
        cost_estimate=pl.CostEstimate(flops=0, bytes_accessed=2**23, transcendentals=0),
        name="pair_products",
    )(place, normed, gain.reshape(1, -1), pair)


def fetch_kernel(place, keys_at, values_at, keys, values, sems):
    copies = [
        pltpu.make_async_copy(keys_at, keys, sems.at[0]),
        pltpu.make_async_copy(values_at, values, sems.at[1]),
    ]
    for copy in copies:
        copy.start()
    for copy in copies:
        copy.wait()


def fetch(place, keys, values, after):
    place, _ = lax.optimization_barrier((place, after))
    return pl.pallas_call(
        fetch_kernel,
        out_shape=[jax.ShapeDtypeStruct(x.shape, x.dtype) for x in (keys, values)],
        in_specs=[smem()] + [pl.BlockSpec(memory_space=pl.ANY)] * 2,
        out_specs=[vmem(), vmem()],
        scratch_shapes=[pltpu.SemaphoreType.DMA((2,))],
        compiler_params=params(1),
        cost_estimate=pl.CostEstimate(flops=0, bytes_accessed=2**22, transcendentals=0),
        name="fetch",
    )(place, keys, values)


def norm_kernel(place, e0, e1, e2, e3, gain, normed, own):
    t = place[0]
    count, width = own.shape
    blocks = [e[:count, :].astype(jnp.float32) for e in (e0, e1, e2, e3)]
    square = sum(jnp.sum(b * b, axis=1, keepdims=True) for b in blocks)
    scale = lax.rsqrt(square / D + EPSILON)
    for k, block in enumerate(blocks):
        columns = pl.ds(pl.multiple_of((t ^ k) * width, width), width)
        value = (block * scale * gain[:, columns]).astype(jnp.bfloat16)
        normed[:, columns] = value
        if k == 0:
            own[...] = value


def norm(place, blocks, gain, count):
    width = blocks[0].shape[1]
    return pl.pallas_call(
        norm_kernel,
        out_shape=(
            jax.ShapeDtypeStruct((count, 4 * width), jnp.bfloat16),
            jax.ShapeDtypeStruct((count, width), jnp.bfloat16),
        ),
        in_specs=[smem()] + [vmem()] * 5,
        out_specs=(vmem(), vmem()),
        compiler_params=params(8),
        name="norm",
    )(place, *blocks, gain.reshape(1, -1))


def products_kernel(own, sums, got, out):
    count = own.shape[0]
    half = sums.shape[2]

    def combine(parts):
        left = sum(dot_nt(own[:, :half], p) for p in parts)
        right = sum(dot_nt(own[:, half:], p) for p in parts)
        lane = lax.broadcasted_iota(jnp.int32, left.shape, 1)
        mixed = jnp.where(lane % 2 == 0, left, right)
        mixed = mixed + pltpu.roll(mixed, mixed.shape[1] - 1, 1)
        return jnp.where((lane % 8 == 0) | (lane % 8 == 2), mixed, 0.0)

    rows = sums[...].reshape(-1, half)
    old = combine([got[:, :, 3 * half :].reshape(-1, half)])
    new = combine(split(rows))
    out[:count, :] = new + pltpu.roll(old, 1, 1)
    out[count:, :] = jnp.full((8, rows.shape[0]), jnp.sum(rows * rows), jnp.float32)


def products(own, sums, got):
    count = own.shape[0]
    return pl.pallas_call(
        products_kernel,
        out_shape=jax.ShapeDtypeStruct((count + 8, sums.shape[0] * 8), jnp.float32),
        in_specs=[vmem()] * 3,
        out_specs=vmem(),
        compiler_params=params(8),
        name="products",
    )(own, sums, got)


def attend_kernel(
    place, base_query, p0, p1, p2, p3, sums, got, gain, key_new, value_new, s0, s1, s2,
    s3, own_sum, old_down, old_up, keys, values, out, new_down, new_up, queries, results,
):
    t = place[0]
    rows_here = keys.shape[0]
    count, width = base_query.shape
    heads = width // HEAD
    steps = count // rows_here
    per_row = steps * heads
    half = width // 2

    both = (p0[...] + p1[...]) + (p2[...] + p3[...])
    product = both[:count, :]
    overall = both[count : count + 1, :]
    clip = RATE * (1.0 / jnp.maximum(jnp.sqrt(overall), 1.0))
    lanes = product.shape[1]
    lane = lax.broadcasted_iota(jnp.int32, product.shape, 1) % 8
    updated = pltpu.roll(product, lanes - 1, 1) - clip * product
    updated = jnp.where((lane == 0) | (lane == 2), updated, 0.0)
    clip = clip[:, :1]
    old = got[:, :, 3 * half :].astype(jnp.float32)
    rows = (old - clip[None] * sums[...]).reshape(-1, half)
    row_high, row_low = split(rows)
    for h in (0, 1):
        left_high, left_low = split(pltpu.roll(updated, 4 + h, 1))
        change = dot_nn(left_high, row_high) + dot_nn(left_low, row_high)
        change += dot_nn(left_high, row_low)
        query = base_query[:, h * half : (h + 1) * half] + ADAPTER_SCALING * change
        for j in range(heads // 2):
            part = query[:, j * HEAD : (j + 1) * HEAD]
            scale = lax.rsqrt(jnp.mean(part * part, axis=1, keepdims=True) + EPSILON)
            part = (part * scale * gain[...]).astype(jnp.bfloat16).astype(jnp.float32)
            for s in range(steps):
                at = s * heads + h * (heads // 2) + j
                queries[pl.ds(at, rows_here, stride=per_row), :] = part[
                    s * rows_here : (s + 1) * rows_here
                ]

    inverse = 1.0 / math.sqrt(HEAD)
    new_lane = lax.broadcasted_iota(jnp.int32, (per_row, count), 1)
    step = lax.broadcasted_iota(jnp.int32, (per_row, count), 0) // heads
    seen = new_lane // rows_here <= step
    query = queries[...].astype(jnp.bfloat16)
    own = [slice(row * per_row, (row + 1) * per_row) for row in range(rows_here)]
    fresh = dot_nt(query, key_new[...]) * inverse
    old, new = [], []
    for row in range(rows_here):
        old.append(dot_nn(query[own[row]], keys[row]) * inverse)
        new.append(jnp.where((new_lane % rows_here == row) & seen, fresh[own[row]], -jnp.inf))
    for row in range(rows_here):
        top = jnp.maximum(
            jnp.max(old[row], axis=1, keepdims=True), jnp.max(new[row], axis=1, keepdims=True)
        )
        old[row], new[row] = jnp.exp(old[row] - top), jnp.exp(new[row] - top)
    for row in range(rows_here):
        total = jnp.sum(old[row], axis=1, keepdims=True) + jnp.sum(new[row], axis=1, keepdims=True)
        share = 1.0 / total
        old[row] = (old[row] * share).astype(jnp.bfloat16)
        new[row] = (new[row] * share).astype(jnp.bfloat16)
    for row in range(rows_here):
        results[own[row], :] = dot_nn(old[row], values[row]) + dot_nn(new[row], value_new[...])

    for h in range(heads):
        parts = [results[pl.ds(s * heads + h, rows_here, stride=per_row), :] for s in range(steps)]
        out[:, h * HEAD : (h + 1) * HEAD] = jnp.concatenate(parts, 0).astype(jnp.bfloat16)

    for k, block in enumerate((s0, s1, s2, s3)):
        columns = pl.ds(pl.multiple_of((t ^ k) * width, width), width)
        part = block[count : count + 16, :].astype(jnp.float32)
        summed = (part[0:2] + part[2:4]) + part[4:6]
        new_down[:, columns] = old_down[:, columns] - clip * summed
    up = own_sum[...]
    for i in (0, 1):
        for h in (0, 1):
            columns = slice(h * half, (h + 1) * half)
            value = up[4 + 2 * i + h : 5 + 2 * i + h, :]
            new_up[i : i + 1, columns] = old_up[i : i + 1, columns] - clip * value


def attend(place, *arrays):
    base_query = arrays[0]
    count, width = base_query.shape
    old_down, old_up = arrays[-4:-2]
    return pl.pallas_call(
        attend_kernel,
        out_shape=(
            jax.ShapeDtypeStruct((count, width), jnp.bfloat16),
            jax.ShapeDtypeStruct(old_down.shape, jnp.float32),
            jax.ShapeDtypeStruct(old_up.shape, jnp.float32),
        ),
        in_specs=[smem()] + [vmem()] * len(arrays),
        out_specs=(vmem(), vmem(), vmem()),
        scratch_shapes=[
            pltpu.VMEM((count * width // HEAD, HEAD), jnp.float32),
            pltpu.VMEM((count * width // HEAD, HEAD), jnp.float32),
        ],
        compiler_params=params(16),
        name="attend",
    )(place, *arrays)


def tensor_swap(values, bit):
    size = lax.axis_size("tensor")
    return lax.ppermute(values, "tensor", [(i, i ^ bit) for i in range(size)])


def body(
    token_ids,
    embed_table,
    norm_gain,
    query_gain,
    key_gain,
    base_query_weight,
    pair_weight,
    past_pairs,
    down_factor,
    up_factor,
    grad_down,
    grad_up,
    group_scale,
    learner_group,
):
    groups = lax.axis_size("dp")
    t = lax.axis_index("tensor")
    me = lax.axis_index("dp")
    width = embed_table.shape[1]
    half = width // 2
    pair_index = t * (width // HEAD) // (HEADS // KVH)
    place = jnp.stack([t, pair_index, me]).astype(jnp.int32)
    rows_here, context = past_pairs.shape[:2]
    steps = token_ids.shape[0]
    count = steps * rows_here

    sent, pick, rounds = send(
        place, token_ids, embed_table, grad_down, grad_up, down_factor, up_factor, groups
    )
    got = lax.all_to_all(sent.reshape(groups, CAP, -1), "dp", 0, 0, tiled=True)

    def later_round(state):
        r, rows = state
        sent, pick = again(place, (r * CAP).reshape(1), token_ids, embed_table, groups)
        for k in range(groups):
            there, source = (me + k) % groups * CAP, (me - k) % groups * CAP
            part = lax.dynamic_slice_in_dim(sent, there, CAP, 0)
            if k:
                ring = [(i, (i + k) % groups) for i in range(groups)]
                part = lax.ppermute(part, "dp", ring)
            wanted = lax.dynamic_slice_in_dim(pick, source, CAP, 0)
            found = lax.dot_general(
                wanted, part, (((0,), (0,)), ((), ())), preferred_element_type=jnp.float32
            )
            rows = rows + found.astype(jnp.bfloat16)
        return r + 1, rows

    _, extra = lax.while_loop(
        lambda s: s[0] < rounds[0],
        later_round,
        (jnp.int32(1), jnp.zeros((count, width), jnp.bfloat16)),
    )
    cache = past_pairs.reshape(rows_here, context, KVH, 2, HEAD).transpose(0, 1, 3, 2, 4)
    cache = cache.reshape(rows_here, context * KVH * 2, HEAD)
    keys, values = stage(place, cache, pick)
    pick, keys, values = lax.optimization_barrier((pick, keys, values))
    block, own_sum, sums = gather(group_scale, learner_group, got, pick, extra)
    sums = lax.all_to_all(sums, "dp", 0, 0, tiled=True)

    blocks = [block] + [tensor_swap(block, bit) for bit in (1, 2, 3)]
    normed, own = norm(place, blocks, norm_gain, count)

    key_new, value_new = pair_products(place, normed, key_gain, pair_weight)
    query = jnp.dot(normed, base_query_weight, preferred_element_type=jnp.float32)
    own, query, key_new = lax.optimization_barrier((own, query, key_new))

    part = products(own, sums, got)
    keys, values = fetch(place, keys, values, part)
    parts = [part] + [tensor_swap(part, bit) for bit in (1, 2, 3)]
    attended, new_down, new_up = attend(
        place, query, *parts, sums, got, query_gain.reshape(1, -1), key_new, value_new,
        *blocks, own_sum, down_factor, up_factor, keys, values,
    )
    return attended.reshape(steps, rows_here, width), new_down, new_up


def solution(mesh):
    in_specs = (
        P(),
        P("dp", "tensor"),
        P(),
        P(),
        P(),
        P(None, "tensor"),
        P(),
        P("dp", None, None, None),
        P("dp", None),
        P("dp", "tensor"),
        P("dp", None, None),
        P("dp", None, "tensor"),
        P(),
        P(),
    )
    out_specs = (P(None, "dp", "tensor"), P("dp", None), P("dp", "tensor"))
    return jax.shard_map(body, mesh=mesh, in_specs=in_specs, out_specs=out_specs, check_vma=False)
```

```python
import math

import jax
import jax.numpy as jnp
from jax import lax
from jax.experimental import pallas as pl
from jax.experimental.pallas import tpu as pltpu
from jax.sharding import PartitionSpec as P

D = 4096
HEAD = 128
HEADS = 32
KVH = 2
R = 64
STEPS = 4
HD = 4096
CAP = 8

TABLE_PARTS = 2

EPSILON = 1e-06
STEP_RATIO = 0.3
ADAPTER_SCALING = 1.0 / 1024.0
RATE = STEP_RATIO * math.sqrt(R * (D + HD))
MIB = 1024 * 1024


def split(values):
    high = values.astype(jnp.bfloat16)
    return high, (values - high.astype(jnp.float32)).astype(jnp.bfloat16)


def thirds(values):
    first, _ = split(values)
    second, third = split(values - first.astype(jnp.float32))
    return first, second, third


def dot_nt(a, b):
    return lax.dot_general(a, b, (((1,), (1,)), ((), ())), preferred_element_type=jnp.float32)


def dot_nn(a, b):
    return lax.dot_general(a, b, (((1,), (0,)), ((), ())), preferred_element_type=jnp.float32)


def vmem():
    return pl.BlockSpec(memory_space=pltpu.VMEM)


def smem():
    return pl.BlockSpec(memory_space=pltpu.SMEM)


def whole(x):
    return pl.BlockSpec(x.shape, lambda *_: (0,) * len(x.shape))


def params(mib):
    return pltpu.CompilerParams(vmem_limit_bytes=mib * MIB)


def fold(down, up):
    half = down.shape[1] // 2
    rows = [x[i : i + 1, h * half : (h + 1) * half] for x in (down, up) for i in (0, 1) for h in (0, 1)]
    return jnp.concatenate(rows, axis=0)


def arrange_ids(tokens, groups):
    steps, rows = tokens.shape
    here = rows // groups
    row = lax.broadcasted_iota(jnp.int32, (groups, rows), 0)
    lane = lax.broadcasted_iota(jnp.int32, (groups, rows), 1)
    parts = []
    for s in range(steps):
        own = jnp.where(lane // here == row, jnp.broadcast_to(tokens[s : s + 1], lane.shape), 0)
        parts.append(own)
    wide = jnp.concatenate(parts, axis=1)
    pieces = jnp.concatenate([wide & 255, (wide >> 8) & 255, wide >> 16], axis=0)
    pieces = pieces.astype(jnp.float32).astype(jnp.bfloat16)
    source = lax.broadcasted_iota(jnp.int32, (steps * rows, 128), 0)
    target = lax.broadcasted_iota(jnp.int32, (steps * rows, 128), 1) % (steps * here)
    same = (source % here == target % here) & (source // rows == target // here)
    ids = dot_nn(pieces, jnp.where(same, 1.0, 0.0).astype(jnp.bfloat16)).astype(jnp.int32)
    return ids[:groups] + (ids[groups : 2 * groups] << 8) + (ids[2 * groups :] << 16)


def find_rows(place, first, ids, table, period, pick, places):
    groups, lanes = ids.shape
    vocab_rows = table.shape[0]
    lane = lax.broadcasted_iota(jnp.int32, ids.shape, 1) % period
    owner = ((ids.astype(jnp.float32) + 0.5) * (1.0 / vocab_rows)).astype(jnp.int32)
    lowest = owner * vocab_rows
    repeated = jnp.zeros(ids.shape, jnp.int32)
    for k in range(1, period):
        repeated = jnp.where((pltpu.roll(ids, k, 1) == ids) & (lane >= k), 1, repeated)
    distinct = jnp.where(repeated == 0, ids, -1)
    slot = jnp.zeros(ids.shape, jnp.int32)
    for k in range(1, period):
        other = pltpu.roll(distinct, k, 1)
        slot += jnp.where((other >= lowest) & (other < ids), 1, 0)
    rounds = jnp.max(slot) // CAP + 1
    slot -= first
    places[...] = jnp.where((slot >= 0) & (slot < CAP), owner * CAP + slot, -1)

    me = place[2]
    own = places[pl.ds(me, 1), :]
    rows = groups * CAP
    at = lax.broadcasted_iota(jnp.int32, (rows, lanes), 0)
    pick[...] = jnp.where(at == own, 1.0, 0.0).astype(jnp.bfloat16)[:, :period]

    local = jnp.where(owner == me, ids - lowest, -1)
    spread = (groups, CAP, lanes)
    local = jnp.broadcast_to(local[:, None, :], spread).reshape(rows, lanes)
    slot = jnp.broadcast_to(slot[:, None, :], spread).reshape(rows, lanes)
    wanted = lax.broadcasted_iota(jnp.int32, (rows, lanes), 0) % CAP
    chosen = jnp.max(jnp.where(slot == wanted, local, -1), axis=1, keepdims=True)
    return chosen, rounds


def one_hot(chosen, vocab_rows):
    at = lax.broadcasted_iota(jnp.int32, (chosen.shape[0], vocab_rows), 1)
    return jnp.where(at == chosen, 1.0, 0.0).astype(jnp.bfloat16)


def read_rows(hot, table):
    main = hot.shape[1] // 256 * 256
    found = dot_nn(hot[:, :main], table[:main, :])
    if main < hot.shape[1]:
        found += dot_nn(hot[:, main:], table[main:, :])
    return found.astype(jnp.bfloat16)


def send_kernel(
    place, tokens_at, table_at, grad_down_at, grad_up_at, sent, pick, rounds,
    tokens, table, grad_down, grad_up, places, sems,
):
    groups = sent.shape[0] // CAP
    vocab_rows, width = table.shape
    half = width // 2
    ranks = grad_up.shape[1]
    columns = pl.ds(pl.multiple_of(place[0] * width, width), width)
    copies = [
        pltpu.make_async_copy(source, target, sems.at[i])
        for i, (source, target) in enumerate(
            (
                (tokens_at, tokens),
                (grad_down_at.at[:, :, columns], grad_down),
                (grad_up_at, grad_up),
            )
        )
    ]
    span = width // TABLE_PARTS
    spans = [slice(i * span, (i + 1) * span) for i in range(TABLE_PARTS)]
    copies += [
        pltpu.make_async_copy(table_at.at[:, at], table.at[:, at], sems.at[3 + i])
        for i, at in enumerate(spans)
    ]
    for copy in copies:
        copy.start()
    copies[0].wait()
    ids = arrange_ids(tokens[...], groups)
    chosen, count = find_rows(place, 0, ids, table, pick.shape[1], pick, places)
    rounds[0] = count
    for copy in copies[1:3]:
        copy.wait()

    grads = jnp.concatenate([grad_down[0], grad_up[0]], axis=0)
    row = lax.broadcasted_iota(jnp.int32, (groups * 8, 2 * ranks), 0)
    source = lax.broadcasted_iota(jnp.int32, (groups * 8, 2 * ranks), 1)
    wanted = row // 4 % 2 * ranks + row // 8 * 2 + row // 2 % 2
    moved = jnp.zeros((groups * 8, half), jnp.float32)
    for h in (0, 1):
        taken = jnp.where((source == wanted) & (row % 2 == h), 1.0, 0.0).astype(jnp.bfloat16)
        moved += dot_nn(taken, grads[:, h * half : (h + 1) * half])
    sent[:, width:] = moved.astype(jnp.bfloat16)

    hot = one_hot(chosen, vocab_rows)
    for i, at in enumerate(spans):
        copies[3 + i].wait()
        sent[:, at] = read_rows(hot, table.at[:, at])


def send(place, tokens, table, grad_down, grad_up, groups):
    width = table.shape[1]
    count = tokens.size // groups
    anywhere = pl.BlockSpec(memory_space=pl.ANY)
    return pl.pallas_call(
        send_kernel,
        out_shape=(
            jax.ShapeDtypeStruct((groups * CAP, width * 3 // 2), jnp.bfloat16),
            jax.ShapeDtypeStruct((groups * CAP, count), jnp.bfloat16),
            jax.ShapeDtypeStruct((1,), jnp.int32),
        ),
        in_specs=[smem()] + [anywhere] * 4,
        out_specs=(vmem(), vmem(), smem()),
        scratch_shapes=[
            pltpu.VMEM(tokens.shape, jnp.int32),
            pltpu.VMEM(table.shape, jnp.bfloat16),
            pltpu.VMEM(grad_up.shape, jnp.bfloat16),
            pltpu.VMEM(grad_up.shape, jnp.bfloat16),
            pltpu.VMEM((groups, 128), jnp.int32),
            pltpu.SemaphoreType.DMA((3 + TABLE_PARTS,)),
        ],
        compiler_params=params(56),
        name="send",
    )(place, tokens, table, grad_down, grad_up)


def again_kernel(place, first, tokens, table, sent, pick, places):
    groups = sent.shape[0] // CAP
    ids = arrange_ids(tokens[...], groups)
    chosen, _ = find_rows(place, first[0], ids, table, pick.shape[1], pick, places)
    sent[...] = read_rows(one_hot(chosen, table.shape[0]), table)


def again(place, first, tokens, table, groups):
    return pl.pallas_call(
        again_kernel,
        out_shape=(
            jax.ShapeDtypeStruct((groups * CAP, table.shape[1]), jnp.bfloat16),
            jax.ShapeDtypeStruct((groups * CAP, tokens.size // groups), jnp.bfloat16),
        ),
        in_specs=[smem(), smem(), vmem(), vmem()],
        out_specs=(vmem(), vmem()),
        scratch_shapes=[pltpu.VMEM((groups, 128), jnp.int32)],
        compiler_params=params(20),
        name="again",
    )(place, first, tokens, table)


def gather_kernel(place, scale, learner, got, pick, extra, down, up, block, own_sum, sent):
    groups = got.shape[0]
    count, width = extra.shape
    half = width // 2
    total = jnp.zeros((8, half), jnp.float32)
    for learn in range(groups):
        weight = scale[learner[learn]]
        total += got[learn, :, width : width + half].astype(jnp.float32) * weight
    own_sum[...] = total
    columns = pl.ds(pl.multiple_of(place[0] * width, width), width)
    old = fold(down[:, columns], up[...])
    square = jnp.broadcast_to(jnp.sum(total * total, keepdims=True), (8, 128))
    terms = thirds(square)
    row = lax.broadcasted_iota(jnp.int32, square.shape, 0)
    for i in range(3):
        square = jnp.where(row == i, terms[i].astype(jnp.float32), square)
    square = jnp.where(row < 3, square, 0.0)
    message = jnp.concatenate([total, old, square], axis=1).astype(jnp.bfloat16)
    sent[...] = jnp.broadcast_to(message[None], sent.shape)
    rows = got[:, :, :width].reshape(groups * CAP, width)
    found = lax.dot_general(
        pick[...], rows, (((0,), (0,)), ((), ())), preferred_element_type=jnp.float32
    )
    block[:count, :] = found.astype(jnp.bfloat16) + extra[...]
    own_down = jnp.concatenate(
        [jnp.concatenate([total[2 * i : 2 * i + 1], total[2 * i + 1 : 2 * i + 2]], 1) for i in (0, 1)], 0
    )
    rows = [*thirds(own_down), jnp.zeros((10, width), jnp.bfloat16)]
    block[count:, :] = jnp.concatenate([r.astype(jnp.float32) for r in rows], 0).astype(jnp.bfloat16)


def gather(place, scale, learner, got, pick, extra, down, up):
    groups = got.shape[0]
    count, width = extra.shape
    return pl.pallas_call(
        gather_kernel,
        out_shape=(
            jax.ShapeDtypeStruct((count + 16, width), jnp.bfloat16),
            jax.ShapeDtypeStruct((8, width // 2), jnp.float32),
            jax.ShapeDtypeStruct((groups, 8, width + 128), jnp.bfloat16),
        ),
        in_specs=[smem(), smem(), smem()] + [vmem()] * 5,
        out_specs=(vmem(), vmem(), vmem()),
        compiler_params=params(8),
        name="gather",
    )(place, scale, learner, got, pick, extra, down, up)


def stage_kernel(place, cache_at, keys_at, values_at, cache, keys, values, wide, sems):
    rows, _, count = keys.shape
    copies = [pltpu.make_async_copy(cache_at.at[i], cache.at[i], sems.at[i]) for i in range(rows)]
    for copy in copies:
        copy.start()
    back = []
    for i in range(rows):
        copies[i].wait()
        wide[...] = cache[i].astype(jnp.float32)
        keys[i] = wide[pl.ds(place[1], count, stride=4), :].T.astype(jnp.bfloat16)
        values[i] = wide[pl.ds(place[1] + 2, count, stride=4), :].astype(jnp.bfloat16)
        back.append(pltpu.make_async_copy(keys.at[i], keys_at.at[i], sems.at[rows + 2 * i]))
        back.append(pltpu.make_async_copy(values.at[i], values_at.at[i], sems.at[rows + 2 * i + 1]))
        back[-2].start()
        back[-1].start()
    for copy in back:
        copy.wait()


def stage(place, cache, after):
    rows, entries, _ = cache.shape
    place, _ = lax.optimization_barrier((place, after))
    anywhere = pl.BlockSpec(memory_space=pl.ANY)
    keys = jax.ShapeDtypeStruct((rows, HEAD, entries // 4), jnp.bfloat16)
    values = jax.ShapeDtypeStruct((rows, entries // 4, HEAD), jnp.bfloat16)
    return pl.pallas_call(
        stage_kernel,
        out_shape=[keys, values],
        in_specs=[smem(), anywhere],
        out_specs=[anywhere] * 2,
        scratch_shapes=[
            pltpu.VMEM(cache.shape, jnp.bfloat16),
            pltpu.VMEM(keys.shape, jnp.bfloat16),
            pltpu.VMEM(values.shape, jnp.bfloat16),
            pltpu.VMEM((entries, HEAD), jnp.float32),
            pltpu.SemaphoreType.DMA((3 * rows,)),
        ],
        compiler_params=params(58),
        cost_estimate=pl.CostEstimate(flops=0, bytes_accessed=2**23, transcendentals=0),
        name="stage",
    )(place, cache)


def pair_kernel(place, normed, gain, pair_at, key_new, value_new, pair, sem):
    copy = pltpu.make_async_copy(pair_at.at[place[1]], pair, sem)
    copy.start()
    copy.wait()
    pairs = dot_nn(normed[...], pair[...])
    keys = pairs[:, :HEAD]
    scale = lax.rsqrt(jnp.mean(keys * keys, axis=1, keepdims=True) + EPSILON)
    key_new[...] = (keys * scale * gain[...]).astype(jnp.bfloat16)
    value_new[...] = pairs[:, HEAD:].astype(jnp.bfloat16)


def pair_products(place, normed, gain, pair):
    fresh = jax.ShapeDtypeStruct((normed.shape[0], HEAD), jnp.bfloat16)
    return pl.pallas_call(
        pair_kernel,
        out_shape=(fresh, fresh),
        in_specs=[smem(), vmem(), vmem(), pl.BlockSpec(memory_space=pl.ANY)],
        out_specs=(vmem(), vmem()),
        scratch_shapes=[
            pltpu.VMEM(pair.shape[1:], jnp.bfloat16),
            pltpu.SemaphoreType.DMA(()),
        ],
        compiler_params=params(58),
        cost_estimate=pl.CostEstimate(flops=0, bytes_accessed=2**23, transcendentals=0),
        name="pair_products",
    )(place, normed, gain.reshape(1, -1), pair)


def fetch_kernel(place, keys_at, values_at, keys, values, sems):
    copies = [
        pltpu.make_async_copy(keys_at, keys, sems.at[0]),
        pltpu.make_async_copy(values_at, values, sems.at[1]),
    ]
    for copy in copies:
        copy.start()
    for copy in copies:
        copy.wait()


def fetch(place, keys, values, after):
    place, _ = lax.optimization_barrier((place, after))
    return pl.pallas_call(
        fetch_kernel,
        out_shape=[jax.ShapeDtypeStruct(x.shape, x.dtype) for x in (keys, values)],
        in_specs=[smem()] + [pl.BlockSpec(memory_space=pl.ANY)] * 2,
        out_specs=[vmem(), vmem()],
        scratch_shapes=[pltpu.SemaphoreType.DMA((2,))],
        compiler_params=params(1),
        cost_estimate=pl.CostEstimate(flops=0, bytes_accessed=2**22, transcendentals=0),
        name="fetch",
    )(place, keys, values)


def norm_kernel(place, e0, e1, e2, e3, gain, normed, own):
    t = place[0]
    count, width = own.shape
    blocks = [e[:count, :].astype(jnp.float32) for e in (e0, e1, e2, e3)]
    square = sum(jnp.sum(b * b, axis=1, keepdims=True) for b in blocks)
    scale = lax.rsqrt(square / D + EPSILON)
    for k, block in enumerate(blocks):
        columns = pl.ds(pl.multiple_of((t ^ k) * width, width), width)
        value = (block * scale * gain[:, columns]).astype(jnp.bfloat16)
        normed[:, columns] = value
        if k == 0:
            own[...] = value


def norm(place, blocks, gain, count):
    width = blocks[0].shape[1]
    return pl.pallas_call(
        norm_kernel,
        out_shape=(
            jax.ShapeDtypeStruct((count, 4 * width), jnp.bfloat16),
            jax.ShapeDtypeStruct((count, width), jnp.bfloat16),
        ),
        in_specs=[smem()] + [vmem()] * 5,
        out_specs=(vmem(), vmem()),
        compiler_params=params(8),
        name="norm",
    )(place, *blocks, gain.reshape(1, -1))


def products_kernel(own, rows, out):
    count, width = own.shape
    half = width // 2
    groups = rows.shape[0]

    def combine(part):
        left, right = dot_nt(own[:, :half], part), dot_nt(own[:, half:], part)
        lane = lax.broadcasted_iota(jnp.int32, left.shape, 1)
        mixed = jnp.where(lane % 2 == 0, left, right)
        mixed = mixed + pltpu.roll(mixed, mixed.shape[1] - 1, 1)
        return jnp.where((lane % 8 == 0) | (lane % 8 == 2), mixed, 0.0)

    new = combine(rows[:, :, :half].reshape(groups * 8, half))
    old = combine(rows[:, :, half:width].reshape(groups * 8, half))
    out[:count, :] = new + pltpu.roll(old, 1, 1)
    squares = rows[:, :, width:].astype(jnp.float32).reshape(groups * 8, 128)
    square = jnp.sum(squares, axis=0, keepdims=True)
    out[count:, :] = jnp.broadcast_to(square[:, :1], (8, groups * 8))


def products(own, rows):
    return pl.pallas_call(
        products_kernel,
        out_shape=jax.ShapeDtypeStruct((own.shape[0] + 8, rows.shape[0] * 8), jnp.float32),
        in_specs=[vmem()] * 2,
        out_specs=vmem(),
        compiler_params=params(8),
        name="products",
    )(own, rows)


def attend_kernel(
    place, base_query, p0, p1, p2, p3, factors, gain, key_new, value_new, s0, s1, s2,
    s3, own_sum, old_down, old_up, keys, values, out, new_down, new_up, queries, results,
):
    t = place[0]
    rows_here = keys.shape[0]
    count, width = base_query.shape
    heads = width // HEAD
    steps = count // rows_here
    per_row = steps * heads
    half = width // 2

    both = (p0[...] + p1[...]) + (p2[...] + p3[...])
    product = both[:count, :]
    overall = both[count : count + 1, :]
    clip = RATE * (1.0 / jnp.maximum(jnp.sqrt(overall), 1.0))
    lanes = product.shape[1]
    lane = lax.broadcasted_iota(jnp.int32, product.shape, 1) % 8
    updated = pltpu.roll(product, lanes - 1, 1) - clip * product
    updated = jnp.where((lane == 0) | (lane == 2), updated, 0.0)
    clip = clip[:, :1]
    old = factors[:, :, half:width].astype(jnp.float32)
    rows = (old - clip[None] * factors[:, :, :half].astype(jnp.float32)).reshape(-1, half)
    row_high, row_low = split(rows)
    for h in (0, 1):
        left_high, left_low = split(pltpu.roll(updated, 4 + h, 1))
        change = dot_nn(left_high, row_high) + dot_nn(left_low, row_high)
        change += dot_nn(left_high, row_low)
        query = base_query[:, h * half : (h + 1) * half] + ADAPTER_SCALING * change
        for j in range(heads // 2):
            part = query[:, j * HEAD : (j + 1) * HEAD]
            scale = lax.rsqrt(jnp.mean(part * part, axis=1, keepdims=True) + EPSILON)
            part = (part * scale * gain[...]).astype(jnp.bfloat16).astype(jnp.float32)
            for s in range(steps):
                at = s * heads + h * (heads // 2) + j
                queries[pl.ds(at, rows_here, stride=per_row), :] = part[
                    s * rows_here : (s + 1) * rows_here
                ]

    inverse = 1.0 / math.sqrt(HEAD)
    new_lane = lax.broadcasted_iota(jnp.int32, (per_row, count), 1)
    step = lax.broadcasted_iota(jnp.int32, (per_row, count), 0) // heads
    seen = new_lane // rows_here <= step
    query = queries[...].astype(jnp.bfloat16)
    own = [slice(row * per_row, (row + 1) * per_row) for row in range(rows_here)]
    fresh = dot_nt(query, key_new[...]) * inverse
    old, new = [], []
    for row in range(rows_here):
        old.append(dot_nn(query[own[row]], keys[row]) * inverse)
        new.append(jnp.where((new_lane % rows_here == row) & seen, fresh[own[row]], -jnp.inf))
    for row in range(rows_here):
        top = jnp.maximum(
            jnp.max(old[row], axis=1, keepdims=True), jnp.max(new[row], axis=1, keepdims=True)
        )
        old[row], new[row] = jnp.exp(old[row] - top), jnp.exp(new[row] - top)
    for row in range(rows_here):
        total = jnp.sum(old[row], axis=1, keepdims=True) + jnp.sum(new[row], axis=1, keepdims=True)
        share = 1.0 / total
        old[row] = (old[row] * share).astype(jnp.bfloat16)
        new[row] = (new[row] * share).astype(jnp.bfloat16)
    for row in range(rows_here):
        results[own[row], :] = dot_nn(old[row], values[row]) + dot_nn(new[row], value_new[...])

    for h in range(heads):
        parts = [results[pl.ds(s * heads + h, rows_here, stride=per_row), :] for s in range(steps)]
        out[:, h * HEAD : (h + 1) * HEAD] = jnp.concatenate(parts, 0).astype(jnp.bfloat16)

    for k, block in enumerate((s0, s1, s2, s3)):
        columns = pl.ds(pl.multiple_of((t ^ k) * width, width), width)
        part = block[count : count + 16, :].astype(jnp.float32)
        summed = (part[0:2] + part[2:4]) + part[4:6]
        new_down[:, columns] = old_down[:, columns] - clip * summed
    up = own_sum[...]
    for i in (0, 1):
        for h in (0, 1):
            columns = slice(h * half, (h + 1) * half)
            value = up[4 + 2 * i + h : 5 + 2 * i + h, :]
            new_up[i : i + 1, columns] = old_up[i : i + 1, columns] - clip * value


def attend(place, *arrays):
    base_query = arrays[0]
    count, width = base_query.shape
    old_down, old_up = arrays[-4:-2]
    return pl.pallas_call(
        attend_kernel,
        out_shape=(
            jax.ShapeDtypeStruct((count, width), jnp.bfloat16),
            jax.ShapeDtypeStruct(old_down.shape, jnp.float32),
            jax.ShapeDtypeStruct(old_up.shape, jnp.float32),
        ),
        in_specs=[smem()] + [vmem()] * len(arrays),
        out_specs=(vmem(), vmem(), vmem()),
        scratch_shapes=[
            pltpu.VMEM((count * width // HEAD, HEAD), jnp.float32),
            pltpu.VMEM((count * width // HEAD, HEAD), jnp.float32),
        ],
        compiler_params=params(16),
        name="attend",
    )(place, *arrays)


def tensor_swap(values, bit):
    size = lax.axis_size("tensor")
    return lax.ppermute(values, "tensor", [(i, i ^ bit) for i in range(size)])


def body(
    token_ids,
    embed_table,
    norm_gain,
    query_gain,
    key_gain,
    base_query_weight,
    pair_weight,
    past_pairs,
    down_factor,
    up_factor,
    grad_down,
    grad_up,
    group_scale,
    learner_group,
):
    groups = lax.axis_size("dp")
    t = lax.axis_index("tensor")
    me = lax.axis_index("dp")
    width = embed_table.shape[1]
    half = width // 2
    pair_index = t * (width // HEAD) // (HEADS // KVH)
    place = jnp.stack([t, pair_index, me]).astype(jnp.int32)
    rows_here, context = past_pairs.shape[:2]
    steps = token_ids.shape[0]
    count = steps * rows_here

    sent, pick, rounds = send(place, token_ids, embed_table, grad_down, grad_up, groups)
    got = lax.all_to_all(sent.reshape(groups, CAP, -1), "dp", 0, 0, tiled=True)

    def later_round(state):
        r, rows = state
        sent, pick = again(place, (r * CAP).reshape(1), token_ids, embed_table, groups)
        for k in range(groups):
            there, source = (me + k) % groups * CAP, (me - k) % groups * CAP
            part = lax.dynamic_slice_in_dim(sent, there, CAP, 0)
            if k:
                ring = [(i, (i + k) % groups) for i in range(groups)]
                part = lax.ppermute(part, "dp", ring)
            wanted = lax.dynamic_slice_in_dim(pick, source, CAP, 0)
            found = lax.dot_general(
                wanted, part, (((0,), (0,)), ((), ())), preferred_element_type=jnp.float32
            )
            rows = rows + found.astype(jnp.bfloat16)
        return r + 1, rows

    _, extra = lax.while_loop(
        lambda s: s[0] < rounds[0],
        later_round,
        (jnp.int32(1), jnp.zeros((count, width), jnp.bfloat16)),
    )
    cache = past_pairs.reshape(rows_here, context, KVH, 2, HEAD).transpose(0, 1, 3, 2, 4)
    cache = cache.reshape(rows_here, context * KVH * 2, HEAD)
    keys, values = stage(place, cache, pick)
    pick, keys, values = lax.optimization_barrier((pick, keys, values))
    block, own_sum, sums = gather(
        place, group_scale, learner_group, got, pick, extra, down_factor, up_factor
    )
    rows = lax.all_to_all(sums, "dp", 0, 0, tiled=True)

    blocks = [block] + [tensor_swap(block, bit) for bit in (1, 2, 3)]
    normed, own = norm(place, blocks, norm_gain, count)

    key_new, value_new = pair_products(place, normed, key_gain, pair_weight)
    query = jnp.dot(normed, base_query_weight, preferred_element_type=jnp.float32)
    own, query, key_new = lax.optimization_barrier((own, query, key_new))

    part = products(own, rows)
    keys, values = fetch(place, keys, values, part)
    parts = [part] + [tensor_swap(part, bit) for bit in (1, 2, 3)]
    attended, new_down, new_up = attend(
        place, query, *parts, rows, query_gain.reshape(1, -1), key_new, value_new,
        *blocks, own_sum, down_factor, up_factor, keys, values,
    )
    return attended.reshape(steps, rows_here, width), new_down, new_up


def solution(mesh):
    in_specs = (
        P(),
        P("dp", "tensor"),
        P(),
        P(),
        P(),
        P(None, "tensor"),
        P(),
        P("dp", None, None, None),
        P("dp", None),
        P("dp", "tensor"),
        P("dp", None, None),
        P("dp", None, "tensor"),
        P(),
        P(),
    )
    out_specs = (P(None, "dp", "tensor"), P("dp", None), P("dp", "tensor"))
    return jax.shard_map(body, mesh=mesh, in_specs=in_specs, out_specs=out_specs, check_vma=False)
```

```python
import math

import jax
import jax.numpy as jnp
from jax import lax
from jax.experimental import pallas as pl
from jax.experimental.pallas import tpu as pltpu
from jax.sharding import PartitionSpec as P

D = 4096
HEAD = 128
HEADS = 32
KVH = 2
R = 64
STEPS = 4
HD = 4096
CAP = 8

TABLE_PARTS = 2

EPSILON = 1e-06
STEP_RATIO = 0.3
ADAPTER_SCALING = 1.0 / 1024.0
RATE = STEP_RATIO * math.sqrt(R * (D + HD))
MIB = 1024 * 1024


def split(values):
    high = values.astype(jnp.bfloat16)
    return high, (values - high.astype(jnp.float32)).astype(jnp.bfloat16)


def thirds(values):
    first, _ = split(values)
    second, third = split(values - first.astype(jnp.float32))
    return first, second, third


def dot_nt(a, b):
    return lax.dot_general(a, b, (((1,), (1,)), ((), ())), preferred_element_type=jnp.float32)


def dot_nn(a, b):
    return lax.dot_general(a, b, (((1,), (0,)), ((), ())), preferred_element_type=jnp.float32)


def vmem():
    return pl.BlockSpec(memory_space=pltpu.VMEM)


def smem():
    return pl.BlockSpec(memory_space=pltpu.SMEM)


def whole(x):
    return pl.BlockSpec(x.shape, lambda *_: (0,) * len(x.shape))


def params(mib):
    return pltpu.CompilerParams(vmem_limit_bytes=mib * MIB)


def fold(down, up):
    half = down.shape[1] // 2
    rows = [x[i : i + 1, h * half : (h + 1) * half] for x in (down, up) for i in (0, 1) for h in (0, 1)]
    return jnp.concatenate(rows, axis=0)


def arrange_ids(tokens, groups):
    steps, rows = tokens.shape
    here = rows // groups
    row = lax.broadcasted_iota(jnp.int32, (groups, rows), 0)
    lane = lax.broadcasted_iota(jnp.int32, (groups, rows), 1)
    parts = []
    for s in range(steps):
        own = jnp.where(lane // here == row, jnp.broadcast_to(tokens[s : s + 1], lane.shape), 0)
        parts.append(own)
    wide = jnp.concatenate(parts, axis=1)
    pieces = jnp.concatenate([wide & 255, (wide >> 8) & 255, wide >> 16], axis=0)
    pieces = pieces.astype(jnp.float32).astype(jnp.bfloat16)
    source = lax.broadcasted_iota(jnp.int32, (steps * rows, 128), 0)
    target = lax.broadcasted_iota(jnp.int32, (steps * rows, 128), 1) % (steps * here)
    same = (source % here == target % here) & (source // rows == target // here)
    ids = dot_nn(pieces, jnp.where(same, 1.0, 0.0).astype(jnp.bfloat16)).astype(jnp.int32)
    return ids[:groups] + (ids[groups : 2 * groups] << 8) + (ids[2 * groups :] << 16)


def find_rows(place, first, ids, table, period, pick, places):
    groups, lanes = ids.shape
    vocab_rows = table.shape[0]
    lane = lax.broadcasted_iota(jnp.int32, ids.shape, 1) % period
    owner = ((ids.astype(jnp.float32) + 0.5) * (1.0 / vocab_rows)).astype(jnp.int32)
    lowest = owner * vocab_rows
    repeated = jnp.zeros(ids.shape, jnp.int32)
    for k in range(1, period):
        repeated = jnp.where((pltpu.roll(ids, k, 1) == ids) & (lane >= k), 1, repeated)
    distinct = jnp.where(repeated == 0, ids, -1)
    slot = jnp.zeros(ids.shape, jnp.int32)
    for k in range(1, period):
        other = pltpu.roll(distinct, k, 1)
        slot += jnp.where((other >= lowest) & (other < ids), 1, 0)
    rounds = jnp.max(slot) // CAP + 1
    slot -= first
    places[...] = jnp.where((slot >= 0) & (slot < CAP), owner * CAP + slot, -1)

    me = place[2]
    own = places[pl.ds(me, 1), :]
    rows = groups * CAP
    at = lax.broadcasted_iota(jnp.int32, (period, lanes), 0)
    same = at == lax.broadcasted_iota(jnp.int32, (period, lanes), 1)
    own = jnp.max(jnp.where(same, jnp.broadcast_to(own, same.shape), -1), axis=1, keepdims=True)
    at = lax.broadcasted_iota(jnp.int32, (period, rows), 1)
    pick[...] = jnp.where(at == own, 1.0, 0.0).astype(jnp.bfloat16)

    local = jnp.where(owner == me, ids - lowest, -1)
    spread = (groups, CAP, lanes)
    local = jnp.broadcast_to(local[:, None, :], spread).reshape(rows, lanes)
    slot = jnp.broadcast_to(slot[:, None, :], spread).reshape(rows, lanes)
    wanted = lax.broadcasted_iota(jnp.int32, (rows, lanes), 0) % CAP
    chosen = jnp.max(jnp.where(slot == wanted, local, -1), axis=1, keepdims=True)
    return chosen, rounds


def one_hot(chosen, vocab_rows):
    at = lax.broadcasted_iota(jnp.int32, (chosen.shape[0], vocab_rows), 1)
    return jnp.where(at == chosen, 1.0, 0.0).astype(jnp.bfloat16)


def read_rows(hot, table):
    main = hot.shape[1] // 256 * 256
    found = dot_nn(hot[:, :main], table[:main, :])
    if main < hot.shape[1]:
        found += dot_nn(hot[:, main:], table[main:, :])
    return found.astype(jnp.bfloat16)


def send_kernel(
    place, tokens_at, table_at, grad_down_at, grad_up_at, sent, pick, rounds,
    tokens, table, grad_down, grad_up, places, sems,
):
    groups = sent.shape[0] // CAP
    vocab_rows, width = table.shape
    half = width // 2
    ranks = grad_up.shape[1]
    columns = pl.ds(pl.multiple_of(place[0] * width, width), width)
    copies = [
        pltpu.make_async_copy(source, target, sems.at[i])
        for i, (source, target) in enumerate(
            (
                (tokens_at, tokens),
                (grad_down_at.at[:, :, columns], grad_down),
                (grad_up_at, grad_up),
            )
        )
    ]
    span = width // TABLE_PARTS
    spans = [slice(i * span, (i + 1) * span) for i in range(TABLE_PARTS)]
    copies += [
        pltpu.make_async_copy(table_at.at[:, at], table.at[:, at], sems.at[3 + i])
        for i, at in enumerate(spans)
    ]
    for copy in copies:
        copy.start()
    copies[0].wait()
    ids = arrange_ids(tokens[...], groups)
    chosen, count = find_rows(place, 0, ids, table, pick.shape[0], pick, places)
    rounds[0] = count
    for copy in copies[1:3]:
        copy.wait()

    grads = jnp.concatenate([grad_down[0], grad_up[0]], axis=0)
    row = lax.broadcasted_iota(jnp.int32, (groups * 8, 2 * ranks), 0)
    source = lax.broadcasted_iota(jnp.int32, (groups * 8, 2 * ranks), 1)
    wanted = row // 4 % 2 * ranks + row // 8 * 2 + row // 2 % 2
    moved = jnp.zeros((groups * 8, half), jnp.float32)
    for h in (0, 1):
        taken = jnp.where((source == wanted) & (row % 2 == h), 1.0, 0.0).astype(jnp.bfloat16)
        moved += dot_nn(taken, grads[:, h * half : (h + 1) * half])
    sent[:, width:] = moved.astype(jnp.bfloat16)

    hot = one_hot(chosen, vocab_rows)
    for i, at in enumerate(spans):
        copies[3 + i].wait()
        sent[:, at] = read_rows(hot, table.at[:, at])


def send(place, tokens, table, grad_down, grad_up, groups):
    width = table.shape[1]
    count = tokens.size // groups
    anywhere = pl.BlockSpec(memory_space=pl.ANY)
    return pl.pallas_call(
        send_kernel,
        out_shape=(
            jax.ShapeDtypeStruct((groups * CAP, width * 3 // 2), jnp.bfloat16),
            jax.ShapeDtypeStruct((count, groups * CAP), jnp.bfloat16),
            jax.ShapeDtypeStruct((1,), jnp.int32),
        ),
        in_specs=[smem()] + [anywhere] * 4,
        out_specs=(vmem(), vmem(), smem()),
        scratch_shapes=[
            pltpu.VMEM(tokens.shape, jnp.int32),
            pltpu.VMEM(table.shape, jnp.bfloat16),
            pltpu.VMEM(grad_up.shape, jnp.bfloat16),
            pltpu.VMEM(grad_up.shape, jnp.bfloat16),
            pltpu.VMEM((groups, 128), jnp.int32),
            pltpu.SemaphoreType.DMA((3 + TABLE_PARTS,)),
        ],
        compiler_params=params(56),
        name="send",
    )(place, tokens, table, grad_down, grad_up)


def again_kernel(place, first, tokens, table, sent, pick, places):
    groups = sent.shape[0] // CAP
    ids = arrange_ids(tokens[...], groups)
    chosen, _ = find_rows(place, first[0], ids, table, pick.shape[0], pick, places)
    sent[...] = read_rows(one_hot(chosen, table.shape[0]), table)


def again(place, first, tokens, table, groups):
    return pl.pallas_call(
        again_kernel,
        out_shape=(
            jax.ShapeDtypeStruct((groups * CAP, table.shape[1]), jnp.bfloat16),
            jax.ShapeDtypeStruct((tokens.size // groups, groups * CAP), jnp.bfloat16),
        ),
        in_specs=[smem(), smem(), vmem(), vmem()],
        out_specs=(vmem(), vmem()),
        scratch_shapes=[pltpu.VMEM((groups, 128), jnp.int32)],
        compiler_params=params(20),
        name="again",
    )(place, first, tokens, table)


def gather_kernel(place, scale, learner, got, pick, extra, down, up, block, own_sum, sent):
    groups = got.shape[0]
    count, width = extra.shape
    half = width // 2
    total = jnp.zeros((8, half), jnp.float32)
    for learn in range(groups):
        weight = scale[learner[learn]]
        total += got[learn, :, width : width + half].astype(jnp.float32) * weight
    own_sum[...] = total
    columns = pl.ds(pl.multiple_of(place[0] * width, width), width)
    old = fold(down[:, columns], up[...])
    message = jnp.concatenate([total, old], axis=1).astype(jnp.bfloat16)
    sent[...] = jnp.broadcast_to(message[None], sent.shape)
    rows = got[:, :, :width].reshape(groups * CAP, width)
    found = dot_nn(pick[...], rows)
    block[:count, :] = found.astype(jnp.bfloat16) + extra[...]
    own_down = jnp.concatenate(
        [jnp.concatenate([total[2 * i : 2 * i + 1], total[2 * i + 1 : 2 * i + 2]], 1) for i in (0, 1)], 0
    )
    rows = [*thirds(own_down), jnp.zeros((10, width), jnp.bfloat16)]
    block[count:, :] = jnp.concatenate([r.astype(jnp.float32) for r in rows], 0).astype(jnp.bfloat16)


def gather(place, scale, learner, got, pick, extra, down, up):
    groups = got.shape[0]
    count, width = extra.shape
    return pl.pallas_call(
        gather_kernel,
        out_shape=(
            jax.ShapeDtypeStruct((count + 16, width), jnp.bfloat16),
            jax.ShapeDtypeStruct((8, width // 2), jnp.float32),
            jax.ShapeDtypeStruct((groups, 8, width), jnp.bfloat16),
        ),
        in_specs=[smem(), smem(), smem()] + [vmem()] * 5,
        out_specs=(vmem(), vmem(), vmem()),
        compiler_params=params(8),
        name="gather",
    )(place, scale, learner, got, pick, extra, down, up)


def stage_kernel(place, cache_at, keys_at, values_at, cache, keys, values, wide, sems):
    rows, _, count = keys.shape
    copies = [pltpu.make_async_copy(cache_at.at[i], cache.at[i], sems.at[i]) for i in range(rows)]
    for copy in copies:
        copy.start()
    back = []
    for i in range(rows):
        copies[i].wait()
        wide[...] = cache[i].astype(jnp.float32)
        keys[i] = wide[pl.ds(place[1], count, stride=4), :].T.astype(jnp.bfloat16)
        values[i] = wide[pl.ds(place[1] + 2, count, stride=4), :].astype(jnp.bfloat16)
        back.append(pltpu.make_async_copy(keys.at[i], keys_at.at[i], sems.at[rows + 2 * i]))
        back.append(pltpu.make_async_copy(values.at[i], values_at.at[i], sems.at[rows + 2 * i + 1]))
        back[-2].start()
        back[-1].start()
    for copy in back:
        copy.wait()


def stage(place, cache, after):
    rows, entries, _ = cache.shape
    place, _ = lax.optimization_barrier((place, after))
    anywhere = pl.BlockSpec(memory_space=pl.ANY)
    keys = jax.ShapeDtypeStruct((rows, HEAD, entries // 4), jnp.bfloat16)
    values = jax.ShapeDtypeStruct((rows, entries // 4, HEAD), jnp.bfloat16)
    return pl.pallas_call(
        stage_kernel,
        out_shape=[keys, values],
        in_specs=[smem(), anywhere],
        out_specs=[anywhere] * 2,
        scratch_shapes=[
            pltpu.VMEM(cache.shape, jnp.bfloat16),
            pltpu.VMEM(keys.shape, jnp.bfloat16),
            pltpu.VMEM(values.shape, jnp.bfloat16),
            pltpu.VMEM((entries, HEAD), jnp.float32),
            pltpu.SemaphoreType.DMA((3 * rows,)),
        ],
        compiler_params=params(58),
        cost_estimate=pl.CostEstimate(flops=0, bytes_accessed=2**23, transcendentals=0),
        name="stage",
    )(place, cache)


def pair_kernel(place, normed, gain, pair_at, key_new, value_new, pair, sem):
    copy = pltpu.make_async_copy(pair_at.at[place[1]], pair, sem)
    copy.start()
    copy.wait()
    pairs = dot_nn(normed[...], pair[...])
    keys = pairs[:, :HEAD]
    scale = lax.rsqrt(jnp.mean(keys * keys, axis=1, keepdims=True) + EPSILON)
    key_new[...] = (keys * scale * gain[...]).astype(jnp.bfloat16)
    value_new[...] = pairs[:, HEAD:].astype(jnp.bfloat16)


def pair_products(place, normed, gain, pair):
    fresh = jax.ShapeDtypeStruct((normed.shape[0], HEAD), jnp.bfloat16)
    return pl.pallas_call(
        pair_kernel,
        out_shape=(fresh, fresh),
        in_specs=[smem(), vmem(), vmem(), pl.BlockSpec(memory_space=pl.ANY)],
        out_specs=(vmem(), vmem()),
        scratch_shapes=[
            pltpu.VMEM(pair.shape[1:], jnp.bfloat16),
            pltpu.SemaphoreType.DMA(()),
        ],
        compiler_params=params(58),
        cost_estimate=pl.CostEstimate(flops=0, bytes_accessed=2**23, transcendentals=0),
        name="pair_products",
    )(place, normed, gain.reshape(1, -1), pair)


def fetch_kernel(place, keys_at, values_at, keys, values, sems):
    copies = [
        pltpu.make_async_copy(keys_at, keys, sems.at[0]),
        pltpu.make_async_copy(values_at, values, sems.at[1]),
    ]
    for copy in copies:
        copy.start()
    for copy in copies:
        copy.wait()


def fetch(place, keys, values, after):
    place, _ = lax.optimization_barrier((place, after))
    return pl.pallas_call(
        fetch_kernel,
        out_shape=[jax.ShapeDtypeStruct(x.shape, x.dtype) for x in (keys, values)],
        in_specs=[smem()] + [pl.BlockSpec(memory_space=pl.ANY)] * 2,
        out_specs=[vmem(), vmem()],
        scratch_shapes=[pltpu.SemaphoreType.DMA((2,))],
        compiler_params=params(1),
        cost_estimate=pl.CostEstimate(flops=0, bytes_accessed=2**22, transcendentals=0),
        name="fetch",
    )(place, keys, values)


def norm_kernel(place, e0, e1, e2, e3, gain, normed, own):
    t = place[0]
    count, width = own.shape
    blocks = [e[:count, :].astype(jnp.float32) for e in (e0, e1, e2, e3)]
    square = sum(jnp.sum(b * b, axis=1, keepdims=True) for b in blocks)
    scale = lax.rsqrt(square / D + EPSILON)
    for k, block in enumerate(blocks):
        columns = pl.ds(pl.multiple_of((t ^ k) * width, width), width)
        value = (block * scale * gain[:, columns]).astype(jnp.bfloat16)
        normed[:, columns] = value
        if k == 0:
            own[...] = value


def norm(place, blocks, gain, count):
    width = blocks[0].shape[1]
    return pl.pallas_call(
        norm_kernel,
        out_shape=(
            jax.ShapeDtypeStruct((count, 4 * width), jnp.bfloat16),
            jax.ShapeDtypeStruct((count, width), jnp.bfloat16),
        ),
        in_specs=[smem()] + [vmem()] * 5,
        out_specs=(vmem(), vmem()),
        compiler_params=params(8),
        name="norm",
    )(place, *blocks, gain.reshape(1, -1))


def products_kernel(own, rows, out):
    count, width = own.shape
    half = width // 2
    groups = rows.shape[0]

    def combine(part):
        left, right = dot_nt(own[:, :half], part), dot_nt(own[:, half:], part)
        lane = lax.broadcasted_iota(jnp.int32, left.shape, 1)
        mixed = jnp.where(lane % 2 == 0, left, right)
        mixed = mixed + pltpu.roll(mixed, mixed.shape[1] - 1, 1)
        return jnp.where((lane % 8 == 0) | (lane % 8 == 2), mixed, 0.0)

    summed = rows[:, :, :half].reshape(groups * 8, half)
    new = combine(summed)
    old = combine(rows[:, :, half:width].reshape(groups * 8, half))
    both = new + pltpu.roll(old, 1, 1)
    lanes = out.shape[1]
    out[:count, :] = both[:, :lanes] + pltpu.roll(both[:, lanes:], 4, 1)
    summed = summed.astype(jnp.float32)
    square = jnp.sum(summed * summed, keepdims=True)
    out[count:, :] = jnp.broadcast_to(square, (8, lanes))


def products(own, rows):
    return pl.pallas_call(
        products_kernel,
        out_shape=jax.ShapeDtypeStruct((own.shape[0] + 8, rows.shape[0] * 4), jnp.float32),
        in_specs=[vmem()] * 2,
        out_specs=vmem(),
        compiler_params=params(8),
        name="products",
    )(own, rows)


def attend_kernel(
    place, base_query, p0, p1, p2, p3, factors, gain, key_new, value_new, s0, s1, s2,
    s3, own_sum, old_down, old_up, keys, values, out, new_down, new_up, queries, results,
):
    t = place[0]
    rows_here = keys.shape[0]
    count, width = base_query.shape
    heads = width // HEAD
    steps = count // rows_here
    per_row = steps * heads
    half = width // 2

    both = (p0[...] + p1[...]) + (p2[...] + p3[...])
    product = both[:count, :]
    overall = both[count : count + 1, :1]
    clip = RATE * (1.0 / jnp.maximum(jnp.sqrt(overall), 1.0))
    lanes = product.shape[1]
    product = jnp.concatenate([product, pltpu.roll(product, lanes - 4, 1)], axis=1)
    lanes = 2 * lanes
    lane = lax.broadcasted_iota(jnp.int32, product.shape, 1) % 8
    updated = pltpu.roll(product, lanes - 1, 1) - clip * product
    updated = jnp.where((lane == 0) | (lane == 2), updated, 0.0)
    dropped = clip * updated
    old = factors[:, :, half:width].reshape(-1, half)
    summed = factors[:, :, :half].reshape(-1, half)
    for h in (0, 1):
        left = jnp.concatenate(split(pltpu.roll(updated, 4 + h, 1)), axis=0)
        less = jnp.concatenate(split(pltpu.roll(dropped, 4 + h, 1)), axis=0)
        change = dot_nn(left, old) - dot_nn(less, summed)
        change = change[:count] + change[count:]
        query = base_query[:, h * half : (h + 1) * half] + ADAPTER_SCALING * change
        for j in range(heads // 2):
            part = query[:, j * HEAD : (j + 1) * HEAD]
            scale = lax.rsqrt(jnp.mean(part * part, axis=1, keepdims=True) + EPSILON)
            part = (part * scale * gain[...]).astype(jnp.bfloat16).astype(jnp.float32)
            for s in range(steps):
                at = s * heads + h * (heads // 2) + j
                queries[pl.ds(at, rows_here, stride=per_row), :] = part[
                    s * rows_here : (s + 1) * rows_here
                ]

    inverse = 1.0 / math.sqrt(HEAD)
    new_lane = lax.broadcasted_iota(jnp.int32, (per_row, count), 1)
    step = lax.broadcasted_iota(jnp.int32, (per_row, count), 0) // heads
    seen = new_lane // rows_here <= step
    query = queries[...].astype(jnp.bfloat16)
    own = [slice(row * per_row, (row + 1) * per_row) for row in range(rows_here)]
    fresh = dot_nt(query, key_new[...]) * inverse
    old, new = [], []
    for row in range(rows_here):
        old.append(dot_nn(query[own[row]], keys[row]) * inverse)
        new.append(jnp.where((new_lane % rows_here == row) & seen, fresh[own[row]], -jnp.inf))
    for row in range(rows_here):
        top = jnp.maximum(
            jnp.max(old[row], axis=1, keepdims=True), jnp.max(new[row], axis=1, keepdims=True)
        )
        old[row], new[row] = jnp.exp(old[row] - top), jnp.exp(new[row] - top)
    for row in range(rows_here):
        total = jnp.sum(old[row], axis=1, keepdims=True) + jnp.sum(new[row], axis=1, keepdims=True)
        share = 1.0 / total
        old[row] = (old[row] * share).astype(jnp.bfloat16)
        new[row] = (new[row] * share).astype(jnp.bfloat16)
    for row in range(rows_here):
        results[own[row], :] = dot_nn(old[row], values[row]) + dot_nn(new[row], value_new[...])

    for h in range(heads):
        parts = [results[pl.ds(s * heads + h, rows_here, stride=per_row), :] for s in range(steps)]
        out[:, h * HEAD : (h + 1) * HEAD] = jnp.concatenate(parts, 0).astype(jnp.bfloat16)

    for k, block in enumerate((s0, s1, s2, s3)):
        columns = pl.ds(pl.multiple_of((t ^ k) * width, width), width)
        part = block[count : count + 16, :].astype(jnp.float32)
        summed = (part[0:2] + part[2:4]) + part[4:6]
        new_down[:, columns] = old_down[:, columns] - clip * summed
    up = own_sum[...]
    for i in (0, 1):
        for h in (0, 1):
            columns = slice(h * half, (h + 1) * half)
            value = up[4 + 2 * i + h : 5 + 2 * i + h, :]
            new_up[i : i + 1, columns] = old_up[i : i + 1, columns] - clip * value


def attend(place, *arrays):
    base_query = arrays[0]
    count, width = base_query.shape
    old_down, old_up = arrays[-4:-2]
    return pl.pallas_call(
        attend_kernel,
        out_shape=(
            jax.ShapeDtypeStruct((count, width), jnp.bfloat16),
            jax.ShapeDtypeStruct(old_down.shape, jnp.float32),
            jax.ShapeDtypeStruct(old_up.shape, jnp.float32),
        ),
        in_specs=[smem()] + [vmem()] * len(arrays),
        out_specs=(vmem(), vmem(), vmem()),
        scratch_shapes=[
            pltpu.VMEM((count * width // HEAD, HEAD), jnp.float32),
            pltpu.VMEM((count * width // HEAD, HEAD), jnp.float32),
        ],
        compiler_params=params(16),
        name="attend",
    )(place, *arrays)


def tensor_swap(values, bit):
    size = lax.axis_size("tensor")
    return lax.ppermute(values, "tensor", [(i, i ^ bit) for i in range(size)])


def body(
    token_ids,
    embed_table,
    norm_gain,
    query_gain,
    key_gain,
    base_query_weight,
    pair_weight,
    past_pairs,
    down_factor,
    up_factor,
    grad_down,
    grad_up,
    group_scale,
    learner_group,
):
    groups = lax.axis_size("dp")
    t = lax.axis_index("tensor")
    me = lax.axis_index("dp")
    width = embed_table.shape[1]
    half = width // 2
    pair_index = t * (width // HEAD) // (HEADS // KVH)
    place = jnp.stack([t, pair_index, me]).astype(jnp.int32)
    rows_here, context = past_pairs.shape[:2]
    steps = token_ids.shape[0]
    count = steps * rows_here

    sent, pick, rounds = send(place, token_ids, embed_table, grad_down, grad_up, groups)
    got = lax.all_to_all(sent.reshape(groups, CAP, -1), "dp", 0, 0, tiled=True)

    def later_round(state):
        r, rows = state
        sent, pick = again(place, (r * CAP).reshape(1), token_ids, embed_table, groups)
        for k in range(groups):
            there, source = (me + k) % groups * CAP, (me - k) % groups * CAP
            part = lax.dynamic_slice_in_dim(sent, there, CAP, 0)
            if k:
                ring = [(i, (i + k) % groups) for i in range(groups)]
                part = lax.ppermute(part, "dp", ring)
            found = dot_nn(lax.dynamic_slice_in_dim(pick, source, CAP, 1), part)
            rows = rows + found.astype(jnp.bfloat16)
        return r + 1, rows

    _, extra = lax.while_loop(
        lambda s: s[0] < rounds[0],
        later_round,
        (jnp.int32(1), jnp.zeros((count, width), jnp.bfloat16)),
    )
    cache = past_pairs.reshape(rows_here, context, KVH, 2, HEAD).transpose(0, 1, 3, 2, 4)
    cache = cache.reshape(rows_here, context * KVH * 2, HEAD)
    keys, values = stage(place, cache, pick)
    pick, keys, values = lax.optimization_barrier((pick, keys, values))
    block, own_sum, sums = gather(
        place, group_scale, learner_group, got, pick, extra, down_factor, up_factor
    )
    rows = lax.all_to_all(sums, "dp", 0, 0, tiled=True)

    blocks = [block] + [tensor_swap(block, bit) for bit in (1, 2, 3)]
    normed, own = norm(place, blocks, norm_gain, count)

    key_new, value_new = pair_products(place, normed, key_gain, pair_weight)
    query = jnp.dot(normed, base_query_weight, preferred_element_type=jnp.float32)
    own, query, key_new = lax.optimization_barrier((own, query, key_new))

    part = products(own, rows)
    keys, values = fetch(place, keys, values, part)
    parts = [part] + [tensor_swap(part, bit) for bit in (1, 2, 3)]
    attended, new_down, new_up = attend(
        place, query, *parts, rows, query_gain.reshape(1, -1), key_new, value_new,
        *blocks, own_sum, down_factor, up_factor, keys, values,
    )
    return attended.reshape(steps, rows_here, width), new_down, new_up


def solution(mesh):
    in_specs = (
        P(),
        P("dp", "tensor"),
        P(),
        P(),
        P(),
        P(None, "tensor"),
        P(),
        P("dp", None, None, None),
        P("dp", None),
        P("dp", "tensor"),
        P("dp", None, None),
        P("dp", None, "tensor"),
        P(),
        P(),
    )
    out_specs = (P(None, "dp", "tensor"), P("dp", None), P("dp", "tensor"))
    return jax.shard_map(body, mesh=mesh, in_specs=in_specs, out_specs=out_specs, check_vma=False)
```

```python
import math

import jax
import jax.numpy as jnp
from jax import lax
from jax.experimental import pallas as pl
from jax.experimental.pallas import tpu as pltpu
from jax.sharding import PartitionSpec as P

D = 4096
HEAD = 128
HEADS = 32
KVH = 2
R = 64
STEPS = 4
HD = 4096
CAP = 8

TABLE_PARTS = 2

EPSILON = 1e-06
STEP_RATIO = 0.3
ADAPTER_SCALING = 1.0 / 1024.0
RATE = STEP_RATIO * math.sqrt(R * (D + HD))
MIB = 1024 * 1024


def split(values):
    high = values.astype(jnp.bfloat16)
    return high, (values - high.astype(jnp.float32)).astype(jnp.bfloat16)


def thirds(values):
    first, _ = split(values)
    second, third = split(values - first.astype(jnp.float32))
    return first, second, third


def dot_nt(a, b):
    return lax.dot_general(a, b, (((1,), (1,)), ((), ())), preferred_element_type=jnp.float32)


def dot_nn(a, b):
    return lax.dot_general(a, b, (((1,), (0,)), ((), ())), preferred_element_type=jnp.float32)


def vmem():
    return pl.BlockSpec(memory_space=pltpu.VMEM)


def smem():
    return pl.BlockSpec(memory_space=pltpu.SMEM)


def whole(x):
    return pl.BlockSpec(x.shape, lambda *_: (0,) * len(x.shape))


def params(mib):
    return pltpu.CompilerParams(vmem_limit_bytes=mib * MIB)


def fold(down, up):
    half = down.shape[1] // 2
    rows = [x[i : i + 1, h * half : (h + 1) * half] for x in (down, up) for i in (0, 1) for h in (0, 1)]
    return jnp.concatenate(rows, axis=0)


def arrange_ids(tokens, groups):
    steps, rows = tokens.shape
    here = rows // groups
    row = lax.broadcasted_iota(jnp.int32, (groups, rows), 0)
    lane = lax.broadcasted_iota(jnp.int32, (groups, rows), 1)
    parts = []
    for s in range(steps):
        own = jnp.where(lane // here == row, jnp.broadcast_to(tokens[s : s + 1], lane.shape), 0)
        parts.append(own)
    wide = jnp.concatenate(parts, axis=1)
    pieces = jnp.concatenate([wide & 255, (wide >> 8) & 255, wide >> 16], axis=0)
    pieces = pieces.astype(jnp.float32).astype(jnp.bfloat16)
    source = lax.broadcasted_iota(jnp.int32, (steps * rows, 128), 0)
    target = lax.broadcasted_iota(jnp.int32, (steps * rows, 128), 1) % (steps * here)
    same = (source % here == target % here) & (source // rows == target // here)
    ids = dot_nn(pieces, jnp.where(same, 1.0, 0.0).astype(jnp.bfloat16)).astype(jnp.int32)
    return ids[:groups] + (ids[groups : 2 * groups] << 8) + (ids[2 * groups :] << 16)


def find_rows(place, first, ids, table, period, pick, places):
    groups, lanes = ids.shape
    vocab_rows = table.shape[0]
    lane = lax.broadcasted_iota(jnp.int32, ids.shape, 1) % period
    owner = ((ids.astype(jnp.float32) + 0.5) * (1.0 / vocab_rows)).astype(jnp.int32)
    lowest = owner * vocab_rows
    repeated = jnp.zeros(ids.shape, jnp.int32)
    for k in range(1, period):
        repeated = jnp.where((pltpu.roll(ids, k, 1) == ids) & (lane >= k), 1, repeated)
    distinct = jnp.where(repeated == 0, ids, -1)
    slot = jnp.zeros(ids.shape, jnp.int32)
    for k in range(1, period):
        other = pltpu.roll(distinct, k, 1)
        slot += jnp.where((other >= lowest) & (other < ids), 1, 0)
    rounds = jnp.max(slot) // CAP + 1
    slot -= first
    places[...] = jnp.where((slot >= 0) & (slot < CAP), owner * CAP + slot, -1)

    me = place[2]
    own = places[pl.ds(me, 1), :]
    rows = groups * CAP
    at = lax.broadcasted_iota(jnp.int32, (period, lanes), 0)
    same = at == lax.broadcasted_iota(jnp.int32, (period, lanes), 1)
    own = jnp.max(jnp.where(same, jnp.broadcast_to(own, same.shape), -1), axis=1, keepdims=True)
    at = lax.broadcasted_iota(jnp.int32, (period, rows), 1)
    pick[...] = jnp.where(at == own, 1.0, 0.0).astype(jnp.bfloat16)

    local = jnp.where(owner == me, ids - lowest, -1)
    spread = (groups, CAP, lanes)
    local = jnp.broadcast_to(local[:, None, :], spread).reshape(rows, lanes)
    slot = jnp.broadcast_to(slot[:, None, :], spread).reshape(rows, lanes)
    wanted = lax.broadcasted_iota(jnp.int32, (rows, lanes), 0) % CAP
    chosen = jnp.max(jnp.where(slot == wanted, local, -1), axis=1, keepdims=True)
    return chosen, rounds


def one_hot(chosen, vocab_rows):
    at = lax.broadcasted_iota(jnp.int32, (chosen.shape[0], vocab_rows), 1)
    return jnp.where(at == chosen, 1.0, 0.0).astype(jnp.bfloat16)


def read_rows(hot, table):
    main = hot.shape[1] // 256 * 256
    found = dot_nn(hot[:, :main], table[:main, :])
    if main < hot.shape[1]:
        found += dot_nn(hot[:, main:], table[main:, :])
    return found.astype(jnp.bfloat16)


def send_kernel(
    place, tokens_at, table_at, grad_down_at, grad_up_at, sent, pick, rounds,
    tokens, table, grad_down, grad_up, places, sems,
):
    groups = sent.shape[0] // CAP
    vocab_rows, width = table.shape
    half = width // 2
    ranks = grad_up.shape[1]
    columns = pl.ds(pl.multiple_of(place[0] * width, width), width)
    copies = [
        pltpu.make_async_copy(source, target, sems.at[i])
        for i, (source, target) in enumerate(
            (
                (tokens_at, tokens),
                (grad_down_at.at[:, :, columns], grad_down),
                (grad_up_at, grad_up),
            )
        )
    ]
    span = width // TABLE_PARTS
    spans = [slice(i * span, (i + 1) * span) for i in range(TABLE_PARTS)]
    copies += [
        pltpu.make_async_copy(table_at.at[:, at], table.at[:, at], sems.at[3 + i])
        for i, at in enumerate(spans)
    ]
    for copy in copies:
        copy.start()
    copies[0].wait()
    ids = arrange_ids(tokens[...], groups)
    chosen, count = find_rows(place, 0, ids, table, pick.shape[0], pick, places)
    rounds[0] = count
    for copy in copies[1:3]:
        copy.wait()

    grads = jnp.concatenate([grad_down[0], grad_up[0]], axis=0)
    row = lax.broadcasted_iota(jnp.int32, (groups * 8, 2 * ranks), 0)
    source = lax.broadcasted_iota(jnp.int32, (groups * 8, 2 * ranks), 1)
    wanted = row // 4 % 2 * ranks + row // 8 * 2 + row // 2 % 2
    moved = jnp.zeros((groups * 8, half), jnp.float32)
    for h in (0, 1):
        taken = jnp.where((source == wanted) & (row % 2 == h), 1.0, 0.0).astype(jnp.bfloat16)
        moved += dot_nn(taken, grads[:, h * half : (h + 1) * half])
    sent[:, width:] = moved.astype(jnp.bfloat16)

    hot = one_hot(chosen, vocab_rows)
    for i, at in enumerate(spans):
        copies[3 + i].wait()
        sent[:, at] = read_rows(hot, table.at[:, at])


def send(place, tokens, table, grad_down, grad_up, groups):
    width = table.shape[1]
    count = tokens.size // groups
    anywhere = pl.BlockSpec(memory_space=pl.ANY)
    return pl.pallas_call(
        send_kernel,
        out_shape=(
            jax.ShapeDtypeStruct((groups * CAP, width * 3 // 2), jnp.bfloat16),
            jax.ShapeDtypeStruct((count, groups * CAP), jnp.bfloat16),
            jax.ShapeDtypeStruct((1,), jnp.int32),
        ),
        in_specs=[smem()] + [anywhere] * 4,
        out_specs=(vmem(), vmem(), smem()),
        scratch_shapes=[
            pltpu.VMEM(tokens.shape, jnp.int32),
            pltpu.VMEM(table.shape, jnp.bfloat16),
            pltpu.VMEM(grad_up.shape, jnp.bfloat16),
            pltpu.VMEM(grad_up.shape, jnp.bfloat16),
            pltpu.VMEM((groups, 128), jnp.int32),
            pltpu.SemaphoreType.DMA((3 + TABLE_PARTS,)),
        ],
        compiler_params=params(56),
        name="send",
    )(place, tokens, table, grad_down, grad_up)


def again_kernel(place, first, tokens, table, sent, pick, places):
    groups = sent.shape[0] // CAP
    ids = arrange_ids(tokens[...], groups)
    chosen, _ = find_rows(place, first[0], ids, table, pick.shape[0], pick, places)
    sent[...] = read_rows(one_hot(chosen, table.shape[0]), table)


def again(place, first, tokens, table, groups):
    return pl.pallas_call(
        again_kernel,
        out_shape=(
            jax.ShapeDtypeStruct((groups * CAP, table.shape[1]), jnp.bfloat16),
            jax.ShapeDtypeStruct((tokens.size // groups, groups * CAP), jnp.bfloat16),
        ),
        in_specs=[smem(), smem(), vmem(), vmem()],
        out_specs=(vmem(), vmem()),
        scratch_shapes=[pltpu.VMEM((groups, 128), jnp.int32)],
        compiler_params=params(20),
        name="again",
    )(place, first, tokens, table)


def gather_kernel(place, scale, learner, got, pick, extra, down, up, block, own_sum, sent):
    groups = got.shape[0]
    count, width = extra.shape
    half = width // 2
    total = jnp.zeros((8, half), jnp.float32)
    for learn in range(groups):
        weight = scale[learner[learn]]
        total += got[learn, :, width : width + half].astype(jnp.float32) * weight
    own_sum[...] = total
    columns = pl.ds(pl.multiple_of(place[0] * width, width), width)
    old = fold(down[:, columns], up[...])
    message = jnp.concatenate([total, old], axis=1).astype(jnp.bfloat16)
    sent[...] = jnp.broadcast_to(message[None], sent.shape)
    rows = got[:, :, :width].reshape(groups * CAP, width)
    found = dot_nn(pick[...], rows)
    block[:count, :] = found.astype(jnp.bfloat16) + extra[...]
    own_down = jnp.concatenate(
        [jnp.concatenate([total[2 * i : 2 * i + 1], total[2 * i + 1 : 2 * i + 2]], 1) for i in (0, 1)], 0
    )
    rows = [*thirds(own_down), jnp.zeros((10, width), jnp.bfloat16)]
    block[count:, :] = jnp.concatenate([r.astype(jnp.float32) for r in rows], 0).astype(jnp.bfloat16)


def gather(place, scale, learner, got, pick, extra, down, up):
    groups = got.shape[0]
    count, width = extra.shape
    return pl.pallas_call(
        gather_kernel,
        out_shape=(
            jax.ShapeDtypeStruct((count + 16, width), jnp.bfloat16),
            jax.ShapeDtypeStruct((8, width // 2), jnp.float32),
            jax.ShapeDtypeStruct((groups, 8, width), jnp.bfloat16),
        ),
        in_specs=[smem(), smem(), smem()] + [vmem()] * 5,
        out_specs=(vmem(), vmem(), vmem()),
        compiler_params=params(8),
        name="gather",
    )(place, scale, learner, got, pick, extra, down, up)


def stage_kernel(place, cache_at, keys_at, values_at, cache, keys, values, wide, sems):
    rows, _, count = keys.shape
    copies = [pltpu.make_async_copy(cache_at.at[i], cache.at[i], sems.at[i]) for i in range(rows)]
    for copy in copies:
        copy.start()
    back = []
    for i in range(rows):
        copies[i].wait()
        wide[...] = cache[i].astype(jnp.float32)
        parts = [wide[pl.ds(j, count, stride=4), :] for j in range(4)]
        keys[i] = jnp.where(place[1] == 0, parts[0], parts[1]).T.astype(jnp.bfloat16)
        values[i] = jnp.where(place[1] == 0, parts[2], parts[3]).astype(jnp.bfloat16)
        back.append(pltpu.make_async_copy(keys.at[i], keys_at.at[i], sems.at[rows + 2 * i]))
        back.append(pltpu.make_async_copy(values.at[i], values_at.at[i], sems.at[rows + 2 * i + 1]))
        back[-2].start()
        back[-1].start()
    for copy in back:
        copy.wait()


def stage(place, cache, after):
    rows, entries, _ = cache.shape
    place, _ = lax.optimization_barrier((place, after))
    anywhere = pl.BlockSpec(memory_space=pl.ANY)
    keys = jax.ShapeDtypeStruct((rows, HEAD, entries // 4), jnp.bfloat16)
    values = jax.ShapeDtypeStruct((rows, entries // 4, HEAD), jnp.bfloat16)
    return pl.pallas_call(
        stage_kernel,
        out_shape=[keys, values],
        in_specs=[smem(), anywhere],
        out_specs=[anywhere] * 2,
        scratch_shapes=[
            pltpu.VMEM(cache.shape, jnp.bfloat16),
            pltpu.VMEM(keys.shape, jnp.bfloat16),
            pltpu.VMEM(values.shape, jnp.bfloat16),
            pltpu.VMEM((entries, HEAD), jnp.float32),
            pltpu.SemaphoreType.DMA((3 * rows,)),
        ],
        compiler_params=params(58),
        cost_estimate=pl.CostEstimate(flops=0, bytes_accessed=2**23, transcendentals=0),
        name="stage",
    )(place, cache)


def pair_kernel(place, normed, gain, pair_at, key_new, value_new, pair, sem):
    copy = pltpu.make_async_copy(pair_at.at[place[1]], pair, sem)
    copy.start()
    copy.wait()
    pairs = dot_nn(normed[...], pair[...])
    keys = pairs[:, :HEAD]
    scale = lax.rsqrt(jnp.mean(keys * keys, axis=1, keepdims=True) + EPSILON)
    key_new[...] = (keys * scale * gain[...]).astype(jnp.bfloat16)
    value_new[...] = pairs[:, HEAD:].astype(jnp.bfloat16)


def pair_products(place, normed, gain, pair):
    fresh = jax.ShapeDtypeStruct((normed.shape[0], HEAD), jnp.bfloat16)
    return pl.pallas_call(
        pair_kernel,
        out_shape=(fresh, fresh),
        in_specs=[smem(), vmem(), vmem(), pl.BlockSpec(memory_space=pl.ANY)],
        out_specs=(vmem(), vmem()),
        scratch_shapes=[
            pltpu.VMEM(pair.shape[1:], jnp.bfloat16),
            pltpu.SemaphoreType.DMA(()),
        ],
        compiler_params=params(58),
        cost_estimate=pl.CostEstimate(flops=0, bytes_accessed=2**23, transcendentals=0),
        name="pair_products",
    )(place, normed, gain.reshape(1, -1), pair)


def fetch_kernel(place, keys_at, values_at, keys, values, sems):
    copies = [
        pltpu.make_async_copy(keys_at, keys, sems.at[0]),
        pltpu.make_async_copy(values_at, values, sems.at[1]),
    ]
    for copy in copies:
        copy.start()
    for copy in copies:
        copy.wait()


def fetch(place, keys, values, after):
    place, _ = lax.optimization_barrier((place, after))
    return pl.pallas_call(
        fetch_kernel,
        out_shape=[jax.ShapeDtypeStruct(x.shape, x.dtype) for x in (keys, values)],
        in_specs=[smem()] + [pl.BlockSpec(memory_space=pl.ANY)] * 2,
        out_specs=[vmem(), vmem()],
        scratch_shapes=[pltpu.SemaphoreType.DMA((2,))],
        compiler_params=params(8),
        cost_estimate=pl.CostEstimate(flops=0, bytes_accessed=2**22, transcendentals=0),
        name="fetch",
    )(place, keys, values)


def norm_kernel(place, e0, e1, e2, e3, gain, normed, own):
    t = place[0]
    count, width = own.shape
    blocks = [e[:count, :].astype(jnp.float32) for e in (e0, e1, e2, e3)]
    square = sum(jnp.sum(b * b, axis=1, keepdims=True) for b in blocks)
    scale = lax.rsqrt(square / D + EPSILON)
    for k, block in enumerate(blocks):
        columns = pl.ds(pl.multiple_of((t ^ k) * width, width), width)
        value = (block * scale * gain[:, columns]).astype(jnp.bfloat16)
        normed[:, columns] = value
        if k == 0:
            own[...] = value


def norm(place, blocks, gain, count):
    width = blocks[0].shape[1]
    return pl.pallas_call(
        norm_kernel,
        out_shape=(
            jax.ShapeDtypeStruct((count, 4 * width), jnp.bfloat16),
            jax.ShapeDtypeStruct((count, width), jnp.bfloat16),
        ),
        in_specs=[smem()] + [vmem()] * 5,
        out_specs=(vmem(), vmem()),
        compiler_params=params(8),
        name="norm",
    )(place, *blocks, gain.reshape(1, -1))


def products_kernel(own, rows, out):
    count, width = own.shape
    half = width // 2
    groups = rows.shape[0]

    def combine(part):
        left, right = dot_nt(own[:, :half], part), dot_nt(own[:, half:], part)
        lane = lax.broadcasted_iota(jnp.int32, left.shape, 1)
        mixed = jnp.where(lane % 2 == 0, left, right)
        mixed = mixed + pltpu.roll(mixed, mixed.shape[1] - 1, 1)
        return jnp.where((lane % 8 == 0) | (lane % 8 == 2), mixed, 0.0)

    summed = rows[:, :, :half].reshape(groups * 8, half)
    new = combine(summed)
    old = combine(rows[:, :, half:width].reshape(groups * 8, half))
    both = new + pltpu.roll(old, 1, 1)
    lanes = out.shape[1]
    out[:count, :] = both[:, :lanes] + pltpu.roll(both[:, lanes:], 4, 1)
    summed = summed.astype(jnp.float32)
    square = jnp.sum(summed * summed, keepdims=True)
    out[count:, :] = jnp.broadcast_to(square, (8, lanes))


def products(own, rows):
    return pl.pallas_call(
        products_kernel,
        out_shape=jax.ShapeDtypeStruct((own.shape[0] + 8, rows.shape[0] * 4), jnp.float32),
        in_specs=[vmem()] * 2,
        out_specs=vmem(),
        compiler_params=params(8),
        name="products",
    )(own, rows)


def attend_kernel(
    place, base_query, p0, p1, p2, p3, factors, gain, key_new, value_new, s0, s1, s2,
    s3, own_sum, old_down, old_up, keys, values, out, new_down, new_up, queries, results,
):
    t = place[0]
    rows_here = keys.shape[0]
    count, width = base_query.shape
    heads = width // HEAD
    steps = count // rows_here
    per_row = steps * heads
    half = width // 2

    both = (p0[...] + p1[...]) + (p2[...] + p3[...])
    product = both[:count, :]
    overall = both[count : count + 1, :1]
    clip = RATE * (1.0 / jnp.maximum(jnp.sqrt(overall), 1.0))
    lanes = product.shape[1]
    product = jnp.concatenate([product, pltpu.roll(product, lanes - 4, 1)], axis=1)
    lanes = 2 * lanes
    lane = lax.broadcasted_iota(jnp.int32, product.shape, 1) % 8
    updated = pltpu.roll(product, lanes - 1, 1) - clip * product
    updated = jnp.where((lane == 0) | (lane == 2), updated, 0.0)
    dropped = clip * updated
    old = factors[:, :, half:width].reshape(-1, half)
    summed = factors[:, :, :half].reshape(-1, half)
    for h in (0, 1):
        left = jnp.concatenate(split(pltpu.roll(updated, 4 + h, 1)), axis=0)
        less = jnp.concatenate(split(pltpu.roll(dropped, 4 + h, 1)), axis=0)
        change = dot_nn(left, old) - dot_nn(less, summed)
        change = change[:count] + change[count:]
        query = base_query[:, h * half : (h + 1) * half] + ADAPTER_SCALING * change
        for j in range(heads // 2):
            part = query[:, j * HEAD : (j + 1) * HEAD]
            scale = lax.rsqrt(jnp.mean(part * part, axis=1, keepdims=True) + EPSILON)
            part = (part * scale * gain[...]).astype(jnp.bfloat16).astype(jnp.float32)
            for s in range(steps):
                at = s * heads + h * (heads // 2) + j
                queries[pl.ds(at, rows_here, stride=per_row), :] = part[
                    s * rows_here : (s + 1) * rows_here
                ]

    inverse = 1.0 / math.sqrt(HEAD)
    new_lane = lax.broadcasted_iota(jnp.int32, (per_row, count), 1)
    step = lax.broadcasted_iota(jnp.int32, (per_row, count), 0) // heads
    seen = new_lane // rows_here <= step
    query = queries[...].astype(jnp.bfloat16)
    own = [slice(row * per_row, (row + 1) * per_row) for row in range(rows_here)]
    fresh = dot_nt(query, key_new[...]) * inverse
    old, new = [], []
    for row in range(rows_here):
        old.append(dot_nn(query[own[row]], keys[row]) * inverse)
        new.append(jnp.where((new_lane % rows_here == row) & seen, fresh[own[row]], -jnp.inf))
    for row in range(rows_here):
        top = jnp.maximum(
            jnp.max(old[row], axis=1, keepdims=True), jnp.max(new[row], axis=1, keepdims=True)
        )
        old[row], new[row] = jnp.exp(old[row] - top), jnp.exp(new[row] - top)
    for row in range(rows_here):
        total = jnp.sum(old[row], axis=1, keepdims=True) + jnp.sum(new[row], axis=1, keepdims=True)
        share = 1.0 / total
        old[row] = (old[row] * share).astype(jnp.bfloat16)
        new[row] = (new[row] * share).astype(jnp.bfloat16)
    for row in range(rows_here):
        results[own[row], :] = dot_nn(old[row], values[row]) + dot_nn(new[row], value_new[...])

    for h in range(heads):
        parts = [results[pl.ds(s * heads + h, rows_here, stride=per_row), :] for s in range(steps)]
        out[:, h * HEAD : (h + 1) * HEAD] = jnp.concatenate(parts, 0).astype(jnp.bfloat16)

    for k, block in enumerate((s0, s1, s2, s3)):
        columns = pl.ds(pl.multiple_of((t ^ k) * width, width), width)
        part = block[count : count + 16, :].astype(jnp.float32)
        summed = (part[0:2] + part[2:4]) + part[4:6]
        new_down[:, columns] = old_down[:, columns] - clip * summed
    up = own_sum[...]
    for i in (0, 1):
        for h in (0, 1):
            columns = slice(h * half, (h + 1) * half)
            value = up[4 + 2 * i + h : 5 + 2 * i + h, :]
            new_up[i : i + 1, columns] = old_up[i : i + 1, columns] - clip * value


def attend(place, *arrays):
    base_query = arrays[0]
    count, width = base_query.shape
    old_down, old_up = arrays[-4:-2]
    return pl.pallas_call(
        attend_kernel,
        out_shape=(
            jax.ShapeDtypeStruct((count, width), jnp.bfloat16),
            jax.ShapeDtypeStruct(old_down.shape, jnp.float32),
            jax.ShapeDtypeStruct(old_up.shape, jnp.float32),
        ),
        in_specs=[smem()] + [vmem()] * len(arrays),
        out_specs=(vmem(), vmem(), vmem()),
        scratch_shapes=[
            pltpu.VMEM((count * width // HEAD, HEAD), jnp.float32),
            pltpu.VMEM((count * width // HEAD, HEAD), jnp.float32),
        ],
        compiler_params=params(16),
        name="attend",
    )(place, *arrays)


def tensor_swap(values, bit):
    size = lax.axis_size("tensor")
    return lax.ppermute(values, "tensor", [(i, i ^ bit) for i in range(size)])


def body(
    token_ids,
    embed_table,
    norm_gain,
    query_gain,
    key_gain,
    base_query_weight,
    pair_weight,
    past_pairs,
    down_factor,
    up_factor,
    grad_down,
    grad_up,
    group_scale,
    learner_group,
):
    groups = lax.axis_size("dp")
    t = lax.axis_index("tensor")
    me = lax.axis_index("dp")
    width = embed_table.shape[1]
    half = width // 2
    pair_index = t * (width // HEAD) // (HEADS // KVH)
    place = jnp.stack([t, pair_index, me]).astype(jnp.int32)
    rows_here, context = past_pairs.shape[:2]
    steps = token_ids.shape[0]
    count = steps * rows_here

    sent, pick, rounds = send(place, token_ids, embed_table, grad_down, grad_up, groups)
    got = lax.all_to_all(sent.reshape(groups, CAP, -1), "dp", 0, 0, tiled=True)

    def later_round(state):
        r, rows = state
        sent, pick = again(place, (r * CAP).reshape(1), token_ids, embed_table, groups)
        for k in range(groups):
            there, source = (me + k) % groups * CAP, (me - k) % groups * CAP
            part = lax.dynamic_slice_in_dim(sent, there, CAP, 0)
            if k:
                ring = [(i, (i + k) % groups) for i in range(groups)]
                part = lax.ppermute(part, "dp", ring)
            found = dot_nn(lax.dynamic_slice_in_dim(pick, source, CAP, 1), part)
            rows = rows + found.astype(jnp.bfloat16)
        return r + 1, rows

    _, extra = lax.while_loop(
        lambda s: s[0] < rounds[0],
        later_round,
        (jnp.int32(1), jnp.zeros((count, width), jnp.bfloat16)),
    )
    cache = past_pairs.reshape(rows_here, context, KVH, 2, HEAD).transpose(0, 1, 3, 2, 4)
    cache = cache.reshape(rows_here, context * KVH * 2, HEAD)
    keys, values = stage(place, cache, pick)
    pick, keys, values = lax.optimization_barrier((pick, keys, values))
    block, own_sum, sums = gather(
        place, group_scale, learner_group, got, pick, extra, down_factor, up_factor
    )
    rows = lax.all_to_all(sums, "dp", 0, 0, tiled=True)

    blocks = [block] + [tensor_swap(block, bit) for bit in (1, 2, 3)]
    normed, own = norm(place, blocks, norm_gain, count)

    key_new, value_new = pair_products(place, normed, key_gain, pair_weight)
    query = jnp.dot(normed, base_query_weight, preferred_element_type=jnp.float32)
    own, query, key_new = lax.optimization_barrier((own, query, key_new))

    part = products(own, rows)
    keys, values = fetch(place, keys, values, part)
    parts = [part] + [tensor_swap(part, bit) for bit in (1, 2, 3)]
    attended, new_down, new_up = attend(
        place, query, *parts, rows, query_gain.reshape(1, -1), key_new, value_new,
        *blocks, own_sum, down_factor, up_factor, keys, values,
    )
    return attended.reshape(steps, rows_here, width), new_down, new_up


def solution(mesh):
    in_specs = (
        P(),
        P("dp", "tensor"),
        P(),
        P(),
        P(),
        P(None, "tensor"),
        P(),
        P("dp", None, None, None),
        P("dp", None),
        P("dp", "tensor"),
        P("dp", None, None),
        P("dp", None, "tensor"),
        P(),
        P(),
    )
    out_specs = (P(None, "dp", "tensor"), P("dp", None), P("dp", "tensor"))
    return jax.shard_map(body, mesh=mesh, in_specs=in_specs, out_specs=out_specs, check_vma=False)
```
